256 devices in a mesh: region: 4 (over z_lo), dev: 64 (over y, z_hi, x, core).
Axes of the slice: x: 4, y: 4, z: 8 (z_hi: 2, z_lo: 4; z = z_hi * 4 + z_lo), core: 2. Of those that a mesh axis runs over, the one named last changes fastest.
Arguments:
- disp_start: float32 [3, 5242880], P(None, ('region', 'dev')), may hold values from -6 to 6
- veloc_start: float32 [3, 5242880], P(None, ('region', 'dev')), may hold values from -6 to 6
- jacobian: float32 [3, 125, 81920], P(None, None, ('region', 'dev')), may hold values from 0.5 to 2
- lame_lambda: float32 [125, 81920], P(None, ('region', 'dev')), may hold values from 0.01 to 0.08
- lame_mu: float32 [125, 81920], P(None, ('region', 'dev')), may hold values from 0.01 to 0.08
- density: float32 [125, 81920], P(None, ('region', 'dev')), may hold values from 0.5 to 2
- connect: int32 [125, 81920], P(None, ('region', 'dev')), may hold values from 0 to 20479, as said below
- fine_slots: int32 [20480], P(('region', 'dev')), may hold values from 0 to 320, as said below
- peer_nodes: int32 [4, 655360], P(None, ('region', 'dev')), may hold values from 0 to 2559, as said below
Outputs:
- disp_final: float32 [3, 5242880], P(None, ('region', 'dev'))
- veloc_final: float32 [3, 5242880], P(None, ('region', 'dev'))
The draws below stay inside these ranges and needn't reach their ends.
Inputs may be any that keep to these rules, and one draw needn't show every extreme that they name: `connect`: entry (k, e) is the device-local index of node k of that device's element e; it lies in the window 64 * e to 64 * e + 127 taken modulo 20480; an element's 125 nodes are distinct, and nodes 64 * e to 64 * e + 63 all belong to element e. `fine_slots`: each device's 80 slots first name distinct elements of that device and then hold 320; the two devices whose dev indices differ only in the lowest bit hold 80 fine elements together, and in every draw some device has all 80 slots filled. `peer_nodes`: each row of a device is a permutation of 0 to 2559 that moves an entry only within its aligned group of 128 slots; nodes below 10240 are shared with no other device.
All inputs are finite; a program needn't handle non-finite values.
Results may differ from the reference program's by a relative error of at most 0.0003.
Values sent between devices are 32-bit elements; how exact they have to be, the bound alone decides.
No kernel may reach another device: no remote copies, remote signals or barrier semaphores. Data moves between devices by JAX's collectives and lax.ppermute only.
A program may use at most 128 MiB of HBM per device.

```python
import math
import jax
import jax.numpy as jnp
from jax import lax

NODES = 125
ELEM = 320
NLOC = 20480
FCAP = 80
IFACE = 2560
IGROUP = 128
SUBSTEPS = 4
ELEMS_ALL = 81920
NODES_ALL = 5242880
N_REGION = 4
N_DEV = 64
DEVICES = 256


def draw_connect(key, part):
    key = jax.random.fold_in(key, 11)
    half_win = NLOC // ELEM
    sub_keys = jax.random.split(key, DEVICES * ELEM)

    def one_element(sub_key):
        tail_key, order_key = jax.random.split(sub_key)
        tail = jax.random.permutation(tail_key, half_win)[:NODES - half_win] + half_win
        picked = jnp.concatenate([jnp.arange(half_win, dtype=jnp.int32), tail.astype(jnp.int32)])
        return jax.random.permutation(order_key, picked)
    offsets = jax.vmap(one_element)(sub_keys).reshape(DEVICES, ELEM, NODES)
    starts = (jnp.arange(ELEM, dtype=jnp.int32) * half_win)[None, :, None]
    nodes = (offsets + starts) % NLOC
    return jnp.transpose(nodes, (2, 0, 1)).reshape(NODES, DEVICES * ELEM).astype(jnp.int32)


def draw_fine_slots(key, part):
    key = jax.random.fold_in(key, 23)
    count_key, full_key, order_key = jax.random.split(key, 3)
    pair_count = DEVICES // 2
    even_counts = jax.random.randint(count_key, (pair_count,), 0, FCAP + 1)
    full_pair = jax.random.randint(full_key, (), 0, pair_count)
    even_counts = jnp.where(jnp.arange(pair_count) == full_pair, FCAP, even_counts)
    counts = jnp.stack([even_counts, FCAP - even_counts], axis=1).reshape(DEVICES)
    sub_keys = jax.random.split(order_key, DEVICES)

    def one_device(sub_key):
        return jax.random.permutation(sub_key, ELEM)[:FCAP]
    orders = jax.vmap(one_device)(sub_keys)
    slot_table = jnp.where(jnp.arange(FCAP)[None, :] < counts[:, None], orders, ELEM)
    return slot_table.reshape(DEVICES * FCAP).astype(jnp.int32)


def draw_peer_nodes(key, part):
    key = jax.random.fold_in(key, 37)
    groups = IFACE // IGROUP
    sub_keys = jax.random.split(key, DEVICES * 4 * groups)

    def one_group(sub_key):
        return jax.random.permutation(sub_key, IGROUP)
    orders = jax.vmap(one_group)(sub_keys).reshape(DEVICES, 4, groups, IGROUP)
    offsets = (jnp.arange(groups) * IGROUP)[None, None, :, None]
    values = (orders + offsets).reshape(DEVICES, 4, IFACE)
    return jnp.transpose(values, (1, 0, 2)).reshape(4, DEVICES * IFACE).astype(jnp.int32)


def block_levels(key, extent, shards, low, high):
    factor_of, own = 1.0, jax.random.fold_in(key, 6)
    for position, parts in shards:
        heights = jnp.exp(jax.random.uniform(jax.random.fold_in(own, position), (parts,), jnp.float32, low / len(shards), high / len(shards)))
        factor_of = factor_of * jnp.repeat(heights, extent[position] // parts).reshape([-1 if axis == position else 1 for axis in range(len(extent))])
    return factor_of


def bell_draw(rng, extent, scale, limit, cuts=(), kind=jnp.bfloat16):
    result = scale * jax.random.normal(rng, extent, jnp.float32)
    if cuts:
        result = result * block_levels(rng, extent, cuts, -0.22, 0.18)
    return jnp.clip(result, -limit, limit).astype(kind)


def setup_inputs(seed: int = 0) -> dict:
    seeds = jax.random.split(jax.random.key(seed), 10)
    disp_start = bell_draw(seeds[0], (3, NODES_ALL), 1.0, 6.0, ((1, 256),), jnp.float32)
    veloc_start = bell_draw(seeds[1], (3, NODES_ALL), 1.0, 6.0, ((1, 256),), jnp.float32)
    jacobian = jnp.clip(jnp.exp(math.log(2.0) - 1.3862944 * jax.random.uniform(seeds[2], (3, NODES, ELEMS_ALL), jnp.float32) ** block_levels(seeds[2], (3, NODES, ELEMS_ALL), ((2, 256),), -0.2, 0.2)), 0.5, 2.0)
    lame_lambda = jnp.clip(jnp.exp(math.log(0.08) - 2.0794415 * jax.random.uniform(seeds[3], (NODES, ELEMS_ALL), jnp.float32) ** block_levels(seeds[3], (NODES, ELEMS_ALL), ((1, 256),), -0.2, 0.2)), 0.01, 0.08)
    lame_mu = jnp.clip(jnp.exp(math.log(0.08) - 2.0794415 * jax.random.uniform(seeds[4], (NODES, ELEMS_ALL), jnp.float32) ** block_levels(seeds[4], (NODES, ELEMS_ALL), ((1, 256),), -0.2, 0.2)), 0.01, 0.08)
    density = jnp.clip(jnp.exp(math.log(2.0) - 1.3862944 * jax.random.uniform(seeds[5], (NODES, ELEMS_ALL), jnp.float32) ** block_levels(seeds[5], (NODES, ELEMS_ALL), ((1, 256),), -0.2, 0.2)), 0.5, 2.0)
    connect = draw_connect(jax.random.fold_in(seeds[9], 71), 0)
    fine_slots = draw_fine_slots(jax.random.fold_in(seeds[9], 71), 0)
    peer_nodes = draw_peer_nodes(jax.random.fold_in(seeds[9], 71), 0)
    return {"disp_start": disp_start, "veloc_start": veloc_start, "jacobian": jacobian, "lame_lambda": lame_lambda, "lame_mu": lame_mu, "density": density, "connect": connect, "fine_slots": fine_slots, "peer_nodes": peer_nodes}


GLL_POINTS = (-1.0, -math.sqrt(3.0 / 7.0), 0.0, math.sqrt(3.0 / 7.0), 1.0)
TIME_STEP = 0.2

def slope_rows():
    points = GLL_POINTS
    rows = []
    for row_at in range(5):
        entries = []
        for col_at in range(5):
            if row_at == col_at:
                summed = 0.0
                for other_at in range(5):
                    if other_at != row_at:
                        summed += 1.0 / (points[row_at] - points[other_at])
                entries.append(summed)
            else:
                top_prod = 1.0
                low_prod = 1.0
                for other_at in range(5):
                    if other_at != row_at:
                        top_prod *= points[row_at] - points[other_at]
                    if other_at != col_at:
                        low_prod *= points[col_at] - points[other_at]
                entries.append(top_prod / low_prod / (points[row_at] - points[col_at]))
        rows.append(entries)
    return rows

def slope_stack():
    slopes = jnp.array(slope_rows(), dtype=jnp.float32)
    identity = jnp.eye(5, dtype=jnp.float32)
    along_one = jnp.kron(jnp.kron(slopes, identity), identity)
    along_two = jnp.kron(jnp.kron(identity, slopes), identity)
    along_three = jnp.kron(jnp.kron(identity, identity), slopes)
    return jnp.concatenate([along_one, along_two, along_three], axis=0)

def element_forces(shifted, jac_part, lam_part, mu_part, stacked):
    node_per = shifted.shape[1]
    elements = shifted.shape[2]
    gradients = jnp.einsum('mn,cne->cme', stacked, shifted, precision=lax.Precision.HIGHEST)
    strain = jac_part[None] * gradients.reshape(3, 3, node_per, elements)
    traced = strain[0, 0] + strain[1, 1] + strain[2, 2]
    stress = mu_part[None, None] * (strain + jnp.transpose(strain, (1, 0, 2, 3)))
    stress = stress + jnp.eye(3, dtype=jnp.float32)[:, :, None, None] * (lam_part * traced)[None, None]
    fluxes = (jac_part[None] * stress).reshape(3, 3 * node_per, elements)
    return jnp.einsum('mn,cme->cne', stacked, fluxes, precision=lax.Precision.HIGHEST)

def assemble(values, peer_dev):
    devices, channels, node_count = values.shape
    interior_len = node_count - 4 * IFACE
    interior = values[:, :, :interior_len]
    boundary = values[:, :, interior_len:].reshape(devices, channels, 4, IFACE)
    index_map = jnp.broadcast_to(peer_dev[:, None, :, :], (devices, channels, 4, IFACE)).astype(jnp.int32)
    picked = jnp.take_along_axis(boundary, index_map, axis=3)
    grid_view = picked.reshape(N_REGION, N_DEV, channels, 4, IFACE)
    from_left = jnp.roll(grid_view[:, :, :, 1], 1, axis=1)
    from_right = jnp.roll(grid_view[:, :, :, 0], -1, axis=1)
    from_below = jnp.roll(grid_view[:, :, :, 3], 1, axis=0)
    from_above = jnp.roll(grid_view[:, :, :, 2], -1, axis=0)
    arrived = jnp.stack([from_left, from_right, from_below, from_above], axis=3)
    arrived = arrived.reshape(devices, channels, 4, IFACE)
    inverse = jnp.argsort(index_map, axis=3).astype(jnp.int32)
    placed = jnp.take_along_axis(arrived, inverse, axis=3)
    merged = (boundary + placed).reshape(devices, channels, 4 * IFACE)
    return jnp.concatenate([interior, merged], axis=2)

def reference(disp_start, veloc_start, jacobian, lame_lambda, lame_mu, density, connect, fine_slots, peer_nodes):
    devices = N_REGION * N_DEV
    stacked = slope_stack()
    displace = jnp.transpose(disp_start.reshape(3, devices, NLOC), (1, 0, 2))
    velocity = jnp.transpose(veloc_start.reshape(3, devices, NLOC), (1, 0, 2))
    jac_dev = jnp.transpose(jacobian.reshape(3, NODES, devices, ELEM), (2, 0, 1, 3))
    lam_dev = jnp.transpose(lame_lambda.reshape(NODES, devices, ELEM), (1, 0, 2))
    mu_dev = jnp.transpose(lame_mu.reshape(NODES, devices, ELEM), (1, 0, 2))
    dens_dev = jnp.transpose(density.reshape(NODES, devices, ELEM), (1, 0, 2))
    conn_dev = jnp.transpose(connect.reshape(NODES, devices, ELEM), (1, 0, 2))
    slot_dev = fine_slots.reshape(devices, FCAP)
    peer_dev = jnp.transpose(peer_nodes.reshape(4, devices, IFACE), (1, 0, 2))

    def local_start(pieces):
        disp_one, jac_one, lam_one, mu_one, dens_one, conn_one, slot_one = pieces
        flat_all = conn_one.reshape(-1)
        masses = jnp.zeros((NLOC,), jnp.float32).at[flat_all].add(dens_one.reshape(-1))
        fine_flag = jnp.zeros((ELEM + 1,), jnp.float32).at[slot_one].set(1.0)[:ELEM]
        shifted = jnp.take(disp_one, flat_all, axis=1).reshape(3, NODES, ELEM)
        forces = element_forces(shifted, jac_one, lam_one, mu_one, stacked) * (1.0 - fine_flag)
        coarse = jnp.zeros((3, NLOC), jnp.float32).at[:, flat_all].add(forces.reshape(3, -1))
        return (masses, coarse)

    def local_fine(pieces):
        disp_one, jac_one, lam_one, mu_one, conn_one, slot_one = pieces
        chosen = jnp.minimum(slot_one, ELEM - 1)
        active = (slot_one < ELEM).astype(jnp.float32)
        flat_fine = jnp.take(conn_one, chosen, axis=1).reshape(-1)
        shifted = jnp.take(disp_one, flat_fine, axis=1).reshape(3, NODES, FCAP)
        forces = element_forces(shifted, jnp.take(jac_one, chosen, axis=2), jnp.take(lam_one, chosen, axis=1), jnp.take(mu_one, chosen, axis=1), stacked) * active
        return jnp.zeros((3, NLOC), jnp.float32).at[:, flat_fine].add(forces.reshape(3, -1))
    masses, coarse = lax.map(local_start, (displace, jac_dev, lam_dev, mu_dev, dens_dev, conn_dev, slot_dev))
    masses = assemble(masses[:, None, :], peer_dev)[:, 0, :]
    inv_mass = 1.0 / masses
    coarse = assemble(coarse, peer_dev)
    sub_step = TIME_STEP / SUBSTEPS
    for substep in range(SUBSTEPS):
        fine_sum = assemble(lax.map(local_fine, (displace, jac_dev, lam_dev, mu_dev, conn_dev, slot_dev)), peer_dev)
        velocity = velocity - sub_step * (inv_mass[:, None, :] * (coarse + fine_sum))
        displace = displace + sub_step * velocity
    disp_final = jnp.transpose(displace, (1, 0, 2)).reshape(3, devices * NLOC)
    veloc_final = jnp.transpose(velocity, (1, 0, 2)).reshape(3, devices * NLOC)
    return (disp_final, veloc_final)
```

```python
import math

import jax
import jax.numpy as jnp
import ml_dtypes
import numpy as np
from jax import lax
from jax.experimental import pallas as pl
from jax.experimental.pallas import tpu as pltpu
from jax.sharding import PartitionSpec as P

NODES = 125
ELEM = 320
NLOC = 20480
FCAP = 80
LANES = 128
ROWS = NLOC // LANES
FIRST = ROWS // 2
GROUPS = 20
SHARED = 4 * GROUPS
SUBSTEPS = 4
GLL_POINTS = (-1.0, -math.sqrt(3.0 / 7.0), 0.0, math.sqrt(3.0 / 7.0), 1.0)
TIME_STEP = 0.2
STEP = TIME_STEP / SUBSTEPS
PAD_ROWS = 168
PAD_ELEM = 384


def slope_rows():
    points = GLL_POINTS
    rows = []
    for row_at in range(5):
        entries = []
        for col_at in range(5):
            if row_at == col_at:
                summed = 0.0
                for other_at in range(5):
                    if other_at != row_at:
                        summed += 1.0 / (points[row_at] - points[other_at])
                entries.append(summed)
            else:
                top_prod = 1.0
                low_prod = 1.0
                for other_at in range(5):
                    if other_at != row_at:
                        top_prod *= points[row_at] - points[other_at]
                    if other_at != col_at:
                        low_prod *= points[col_at] - points[other_at]
                entries.append(top_prod / low_prod / (points[row_at] - points[col_at]))
        rows.append(entries)
    return rows


def slope_operands():
    slopes = np.array(slope_rows(), dtype=np.float32)
    eye = np.eye(5, dtype=np.float32)
    along = [
        np.kron(np.kron(slopes, eye), eye),
        np.kron(np.kron(eye, slopes), eye),
        np.kron(np.kron(eye, eye), slopes),
    ]
    grad = np.zeros((LANES, 3 * LANES), np.float32)
    back = np.zeros((3 * LANES, LANES), np.float32)
    for i, matrix in enumerate(along):
        grad[:NODES, i * LANES : i * LANES + NODES] = matrix.T
        back[i * LANES : i * LANES + NODES, :NODES] = matrix

    def terms(whole):
        high = whole.astype(ml_dtypes.bfloat16)
        low = (whole - high.astype(np.float32)).astype(ml_dtypes.bfloat16)
        return np.concatenate([high, high, low], axis=0)

    return terms(grad), terms(back)


def split_terms(whole):
    high = whole.astype(jnp.bfloat16)
    low = (whole - high.astype(jnp.float32)).astype(jnp.bfloat16)
    return high, low


def lane_pick(values, index):
    return jnp.take_along_axis(values, index, axis=1, mode="promise_in_bounds")


def forces(shifted, jac, lam, mu, grad, back):
    count = shifted[0].shape[0]
    high, low = split_terms(jnp.concatenate(shifted, axis=0))
    slope = jnp.dot(
        jnp.concatenate([high, low, high], axis=1), grad, preferred_element_type=jnp.float32
    )
    strain = [
        [
            jac[i] * slope[c * count : (c + 1) * count, i * LANES : (i + 1) * LANES]
            for i in range(3)
        ]
        for c in range(3)
    ]
    traced = lam * (strain[0][0] + strain[1][1] + strain[2][2])
    rows = []
    for c in range(3):
        fluxes = []
        for i in range(3):
            stress = mu * (strain[c][i] + strain[i][c])
            if c == i:
                stress = stress + traced
            fluxes.append(jac[i] * stress)
        rows.append(jnp.concatenate(fluxes, axis=1))
    high, low = split_terms(jnp.concatenate(rows, axis=0))
    out = jnp.dot(
        jnp.concatenate([high, low, high], axis=1), back, preferred_element_type=jnp.float32
    )
    return [out[c * count : (c + 1) * count] for c in range(3)]


def inverse_block(rows_ref, count, missing):
    target = lax.broadcasted_iota(jnp.int32, (LANES, LANES), 0)

    def step(k, found):
        row = rows_ref[pl.ds(k, 1), :]
        return jnp.where(row == target, k, found)

    return lax.fori_loop(
        0, count, step, jnp.full((LANES, LANES), missing, jnp.int32), unroll=4 if count % 4 == 0 else 5
    )


def high_half(shape):
    return lax.broadcasted_iota(jnp.int32, shape, 1) >= LANES // 2


def fine_local(disp_ref, slots_ref, window_ref, statics, spread, grad, back):
    jac0, jac1, jac2, lam, mu, index, place = statics
    upper = high_half((1, LANES))
    for s in range(FCAP):
        e = slots_ref[s]
        first = lax.shift_right_logical(e, 1)
        second = lax.shift_right_logical(e + 1, 1)
        for c in range(3):
            window_ref[c, pl.ds(s, 1), :] = jnp.where(
                upper, disp_ref[c, pl.ds(first, 1), :], disp_ref[c, pl.ds(second, 1), :]
            )
    shifted = [lane_pick(window_ref[c], index) for c in range(3)]
    out = forces(shifted, (jac0, jac1, jac2), lam, mu, grad, back)
    slotted = jnp.concatenate([lane_pick(o, place) for o in out], axis=1)
    upper = lax.broadcasted_iota(jnp.int32, slotted.shape, 1) % LANES >= LANES // 2
    blank = jnp.zeros((LANES - FCAP, slotted.shape[1]), jnp.float32)
    both = jnp.concatenate(
        [jnp.where(upper, slotted, 0.0), blank, jnp.where(upper, 0.0, slotted), blank], axis=0
    )
    high, low = split_terms(both)
    return jnp.dot(spread, high, preferred_element_type=jnp.float32) + jnp.dot(
        spread, low, preferred_element_type=jnp.float32
    )


def send_rows(shared, picks, parities, staged_ref, outs):
    dev_odd, region_odd = parities
    for c, values in enumerate(shared):
        staged_ref[c] = lane_pick(values, picks)
    for c in range(len(shared)):
        part = [staged_ref[c, GROUPS * p : GROUPS * (p + 1), :] for p in range(4)]
        put = pl.ds(c * GROUPS, GROUPS)
        outs[0][put, :] = jnp.where(dev_odd, part[0], part[1])
        outs[1][put, :] = jnp.where(dev_odd, part[1], part[0])
        outs[2][put, :] = jnp.where(region_odd, part[2], part[3])
        outs[3][put, :] = jnp.where(region_odd, part[3], part[2])


def received_rows(arrived, channels, places, parities, staged_ref):
    dev_odd, region_odd = parities
    for c in range(channels):
        got = [a[c * GROUPS : (c + 1) * GROUPS, :] for a in arrived]
        staged_ref[c, 0:GROUPS, :] = jnp.where(dev_odd, got[0], got[1])
        staged_ref[c, GROUPS : 2 * GROUPS, :] = jnp.where(dev_odd, got[1], got[0])
        staged_ref[c, 2 * GROUPS : 3 * GROUPS, :] = jnp.where(region_odd, got[2], got[3])
        staged_ref[c, 3 * GROUPS : 4 * GROUPS, :] = jnp.where(region_odd, got[3], got[2])
    return [lane_pick(staged_ref[c], places) for c in range(channels)]


def own_parities():
    return (
        jnp.bitwise_and(lax.axis_index("dev"), 1) == 1,
        jnp.bitwise_and(lax.axis_index("region"), 1) == 1,
    )


def first_kernel(
    slots_ref,
    slot_row_ref,
    disp_in,
    veloc_in,
    jac_ref,
    lam_ref,
    mu_ref,
    dens_ref,
    conn_ref,
    peer_ref,
    grad_ref,
    back_ref,
    disp_ref,
    veloc_ref,
    coarse_ref,
    summed_ref,
    fixed_ref,
    index_ref,
    spread_ref,
    peer_index_ref,
    sends0,
    sends1,
    sends2,
    sends3,
    turned_ref,
    turned_index_ref,
    pad_ref,
    conn_pad_ref,
    peer_rows_ref,
    peer_cols_ref,
    window_ref,
    staged_ref,
    total_ref,
    spread_wide_ref,
):
    grad, back = grad_ref[...], back_ref[...]
    parities = own_parities()
    for j in range(ROWS):
        cols = slice(j * LANES, (j + 1) * LANES)
        for c in range(3):
            disp_ref[c, j : j + 1, :] = disp_in[c : c + 1, cols]
            veloc_ref[c, j : j + 1, :] = veloc_in[c : c + 1, cols]
    for c in range(3):
        disp_ref[c, ROWS:PAD_ROWS, :] = jnp.broadcast_to(
            disp_in[c : c + 1, 0:LANES], (PAD_ROWS - ROWS, LANES)
        )
    for p in range(4):
        for j in range(GROUPS):
            at = p * GROUPS + j
            peer_rows_ref[at : at + 1, :] = peer_ref[
                p : p + 1, j * LANES : (j + 1) * LANES
            ] & (LANES - 1)
    peer_rows_ref[SHARED:, :] = jnp.zeros((LANES - SHARED, LANES), jnp.int32)
    pad_ref[...] = jnp.zeros_like(pad_ref)
    sources = [jac_ref.at[0], jac_ref.at[1], jac_ref.at[2], lam_ref, mu_ref, dens_ref]
    for a, source in enumerate(sources):
        pad_ref[0:NODES, 0:ELEM] = source[...]
        for b in range(3):
            block = slice(b * LANES, (b + 1) * LANES)
            turned_ref[a, block, :] = pad_ref[:, block].T
    conn_pad_ref[...] = jnp.zeros_like(conn_pad_ref)
    for b in range(3):
        block = slice(b * LANES, (b + 1) * LANES)
        width = min(LANES, ELEM - b * LANES)
        conn_pad_ref[b, 0:NODES, 0:width] = conn_ref[
            :, b * LANES : b * LANES + width
        ] & (LANES - 1)
        turned_index_ref[0, block, :] = conn_pad_ref[b].T
        turned_index_ref[1, block, :] = inverse_block(
            conn_pad_ref.at[b], NODES, LANES - 1
        ).T
    peer_index_ref[0] = peer_rows_ref[0:SHARED, :]
    peer_cols_ref[...] = peer_rows_ref[...].T
    peer_index_ref[1] = inverse_block(peer_cols_ref, LANES, 0).T[0:SHARED, :]
    for s in range(FCAP):
        e = slots_ref[s]
        for a in range(5):
            fixed_ref[a, s : s + 1, :] = turned_ref[a, pl.ds(e, 1), :]
        for a in range(2):
            index_ref[a, s : s + 1, :] = turned_index_ref[a, pl.ds(e, 1), :]
        for a in range(3):
            turned_ref[a, pl.ds(e, 1), :] = jnp.zeros((1, LANES), jnp.float32)
    rows = lax.broadcasted_iota(jnp.int32, (ROWS, FCAP), 0)
    slot_row = slot_row_ref[...]
    second = lax.shift_right_logical(slot_row + 1, 1)
    second = jnp.where(second == ROWS, 0, second)
    spread_wide_ref[...] = jnp.zeros_like(spread_wide_ref)
    spread_wide_ref[:, 0:FCAP] = jnp.where(
        lax.shift_right_logical(slot_row, 1) == rows, 1.0, 0.0
    )
    spread_wide_ref[:, LANES : LANES + FCAP] = jnp.where(second == rows, 1.0, 0.0)
    spread_ref[...] = spread_wide_ref[...].astype(jnp.bfloat16)
    total_ref[...] = jnp.zeros_like(total_ref)
    part = 40
    upper = high_half((1, LANES))
    for r0 in range(0, ROWS, part):

        def paired(ref, a):
            return jnp.concatenate(
                [ref[a, pl.ds(2 * r0 + odd, part, stride=2), :] for odd in range(2)], axis=0
            )

        index, place = paired(turned_index_ref, 0), paired(turned_index_ref, 1)
        shifted = []
        for c in range(3):
            here = disp_ref[c, r0 : r0 + part, :]
            after = disp_ref[c, r0 + 1 : r0 + part + 1, :]
            shifted.append(
                lane_pick(jnp.concatenate([here, jnp.where(upper, here, after)], axis=0), index)
            )
        nodal = forces(
            shifted,
            [paired(turned_ref, a) for a in range(3)],
            paired(turned_ref, 3),
            paired(turned_ref, 4),
            grad,
            back,
        )
        nodal.append(paired(turned_ref, 5))
        for c in range(4):
            spot = lane_pick(nodal[c], place)
            even, odd = spot[:part], spot[part:]
            total_ref[c, r0 : r0 + part, :] += even + jnp.where(upper, odd, 0.0)
            total_ref[c, r0 + 1 : r0 + part + 1, :] += jnp.where(upper, 0.0, odd)
    for c in range(4):
        total_ref[c, 0:1, :] += total_ref[c, ROWS : ROWS + 1, :]
        coarse_ref[c] = total_ref[c, 0:ROWS, :]
    fine = fine_local(
        disp_ref,
        slots_ref,
        window_ref,
        [fixed_ref[a] for a in range(5)] + [index_ref[a] for a in range(2)],
        spread_ref[...],
        grad,
        back,
    )
    for c in range(3):
        summed_ref[c] = coarse_ref[c] + fine[:, c * LANES : (c + 1) * LANES]
    send_rows(
        [summed_ref[c, FIRST:, :] for c in range(3)] + [coarse_ref[3, FIRST:, :]],
        peer_index_ref[0],
        parities,
        staged_ref,
        (sends0, sends1, sends2, sends3),
    )


def advance(disp, veloc, summed_ref, inverse_mass, placed):
    moved = []
    for c in range(3):
        force = jnp.concatenate(
            [summed_ref[c, :FIRST, :], summed_ref[c, FIRST:, :] + placed[c]], axis=0
        )
        v = veloc[c] - STEP * (inverse_mass * force)
        moved.append((disp[c] + STEP * v, v))
    return moved


def middle_kernel(
    opening,
    slots_ref,
    disp_ref,
    veloc_ref,
    coarse_ref,
    summed_ref,
    inverse_ref,
    fixed_ref,
    index_ref,
    spread_ref,
    peer_index_ref,
    got0,
    got1,
    got2,
    got3,
    grad_ref,
    back_ref,
    disp_out,
    veloc_out,
    summed_out,
    *rest,
):
    if opening:
        inverse_out, sends0, sends1, sends2, sends3, window_ref, staged_ref = rest
    else:
        sends0, sends1, sends2, sends3, window_ref, staged_ref = rest
    parities = own_parities()
    placed = received_rows(
        (got0, got1, got2, got3), 4 if opening else 3, peer_index_ref[1], parities, staged_ref
    )
    if opening:
        inverse_out[0:FIRST, :] = 1.0 / coarse_ref[3, 0:FIRST, :]
        inverse_out[FIRST:, :] = 1.0 / (coarse_ref[3, FIRST:, :] + placed[3])
        inverse_mass = inverse_out[...]
    else:
        inverse_mass = inverse_ref[...]
    moved = advance(
        [disp_ref[c, 0:ROWS, :] for c in range(3)],
        [veloc_ref[c] for c in range(3)],
        summed_ref,
        inverse_mass,
        placed,
    )
    for c in range(3):
        disp_out[c, 0:ROWS, :] = moved[c][0]
        disp_out[c, ROWS:PAD_ROWS, :] = jnp.broadcast_to(
            moved[c][0][0:1], (PAD_ROWS - ROWS, LANES)
        )
        veloc_out[c] = moved[c][1]
    fine = fine_local(
        disp_out,
        slots_ref,
        window_ref,
        [fixed_ref[a] for a in range(5)] + [index_ref[a] for a in range(2)],
        spread_ref[...],
        grad_ref[...],
        back_ref[...],
    )
    for c in range(3):
        summed_out[c] = coarse_ref[c] + fine[:, c * LANES : (c + 1) * LANES]
    send_rows(
        [summed_out[c, FIRST:, :] for c in range(3)],
        peer_index_ref[0],
        parities,
        staged_ref,
        (sends0, sends1, sends2, sends3),
    )


def last_kernel(
    disp_ref,
    veloc_ref,
    summed_ref,
    inverse_ref,
    peer_index_ref,
    got0,
    got1,
    got2,
    got3,
    disp_out,
    veloc_out,
    staged_ref,
    rows_ref,
):
    placed = received_rows(
        (got0, got1, got2, got3), 3, peer_index_ref[1], own_parities(), staged_ref
    )
    moved = advance(
        [disp_ref[c, 0:ROWS, :] for c in range(3)],
        [veloc_ref[c] for c in range(3)],
        summed_ref,
        inverse_ref[...],
        placed,
    )
    for which, out in ((0, disp_out), (1, veloc_out)):
        for c in range(3):
            rows_ref[which, c] = moved[c][which]
    for j in range(ROWS):
        cols = slice(j * LANES, (j + 1) * LANES)
        for which, out in ((0, disp_out), (1, veloc_out)):
            for c in range(3):
                out[c : c + 1, cols] = rows_ref[which, c, j : j + 1, :]


def swap_pairs(count, colour):
    pairs = []
    for low in range(colour, count, 2):
        high = (low + 1) % count
        pairs += [(low, high), (high, low)]
    return pairs


def swap_all(sends):
    plan = (("dev", 0), ("dev", 1), ("region", 0), ("region", 1))
    return [
        lax.ppermute(sent, axis, swap_pairs(lax.axis_size(axis), colour))
        for sent, (axis, colour) in zip(sends, plan)
    ]


def shape(dims, kind=jnp.float32):
    return jax.ShapeDtypeStruct(dims, kind)


PARAMS = pltpu.CompilerParams(vmem_limit_bytes=48 * 1024 * 1024)


def body(
    disp_start,
    veloc_start,
    jacobian,
    lame_lambda,
    lame_mu,
    density,
    connect,
    fine_slots,
    peer_nodes,
):
    grad_np, back_np = slope_operands()
    grad, back = jnp.asarray(grad_np), jnp.asarray(back_np)
    scalar = pl.BlockSpec(memory_space=pltpu.SMEM)
    vector = pl.BlockSpec(memory_space=pltpu.VMEM)
    field = shape((3, ROWS, LANES))
    padded = shape((3, PAD_ROWS, LANES))

    def sends(channels):
        return [shape((channels * GROUPS, LANES))] * 4

    outs = pl.pallas_call(
        first_kernel,
        in_specs=[scalar] + [vector] * 11,
        out_shape=[
            padded,
            field,
            shape((4, ROWS, LANES)),
            field,
            shape((5, FCAP, LANES)),
            shape((2, FCAP, LANES), jnp.int32),
            shape((ROWS, 2 * LANES), jnp.bfloat16),
            shape((2, SHARED, LANES), jnp.int32),
        ]
        + sends(4),
        out_specs=[vector] * 12,
        scratch_shapes=[
            pltpu.VMEM((6, PAD_ELEM, LANES), jnp.float32),
            pltpu.VMEM((2, PAD_ELEM, LANES), jnp.int32),
            pltpu.VMEM((LANES, PAD_ELEM), jnp.float32),
            pltpu.VMEM((3, LANES, LANES), jnp.int32),
            pltpu.VMEM((LANES, LANES), jnp.int32),
            pltpu.VMEM((LANES, LANES), jnp.int32),
            pltpu.VMEM((3, FCAP, LANES), jnp.float32),
            pltpu.VMEM((4, SHARED, LANES), jnp.float32),
            pltpu.VMEM((4, PAD_ROWS, LANES), jnp.float32),
            pltpu.VMEM((ROWS, 2 * LANES), jnp.float32),
        ],
        compiler_params=PARAMS,
        name="first",
    )(
        fine_slots,
        fine_slots.reshape(1, FCAP),
        disp_start,
        veloc_start,
        jacobian,
        lame_lambda,
        lame_mu,
        density,
        connect,
        peer_nodes,
        grad,
        back,
    )
    disp, veloc, coarse, summed, fixed, index, spread, peer_index = outs[:8]
    got = swap_all(outs[8:])
    inverse_mass = None
    for substep in range(SUBSTEPS - 1):
        opening = substep == 0
        extra = [shape((ROWS, LANES))] if opening else []
        outs = pl.pallas_call(
            lambda *refs, opening=opening: middle_kernel(opening, *refs),
            in_specs=[scalar] + [vector] * 15,
            out_shape=[padded, field, field] + extra + sends(3),
            out_specs=[vector] * (7 + len(extra)),
            scratch_shapes=[
                pltpu.VMEM((3, FCAP, LANES), jnp.float32),
                pltpu.VMEM((4, SHARED, LANES), jnp.float32),
            ],
            compiler_params=PARAMS,
            name="middle",
        )(
            fine_slots,
            disp,
            veloc,
            coarse,
            summed,
            coarse if opening else inverse_mass,
            fixed,
            index,
            spread,
            peer_index,
            *got,
            grad,
            back,
        )
        disp, veloc, summed = outs[:3]
        if opening:
            inverse_mass = outs[3]
        got = swap_all(outs[-4:])
    return pl.pallas_call(
        last_kernel,
        in_specs=[vector] * 9,
        out_shape=[shape((3, NLOC)), shape((3, NLOC))],
        out_specs=[vector] * 2,
        scratch_shapes=[
            pltpu.VMEM((4, SHARED, LANES), jnp.float32),
            pltpu.VMEM((2, 3, ROWS, LANES), jnp.float32),
        ],
        compiler_params=PARAMS,
        name="last",
    )(disp, veloc, summed, inverse_mass, peer_index, *got)


def solution(mesh):
    in_specs = (
        P(None, ("region", "dev")),
        P(None, ("region", "dev")),
        P(None, None, ("region", "dev")),
        P(None, ("region", "dev")),
        P(None, ("region", "dev")),
        P(None, ("region", "dev")),
        P(None, ("region", "dev")),
        P(("region", "dev")),
        P(None, ("region", "dev")),
    )
    out_specs = (P(None, ("region", "dev")), P(None, ("region", "dev")))
    return jax.shard_map(body, mesh=mesh, in_specs=in_specs, out_specs=out_specs, check_vma=False)
```

```python
import functools
import math

import jax
import jax.numpy as jnp
import ml_dtypes
import numpy as np
from jax import lax
from jax.experimental import pallas as pl
from jax.experimental.pallas import tpu as pltpu
from jax.sharding import PartitionSpec as P

NODES = 125
ELEM = 320
NLOC = 20480
FCAP = 80
LANES = 128
ROWS = NLOC // LANES
FIRST = ROWS // 2
GROUPS = 20
SHARED = 4 * GROUPS
SUBSTEPS = 4
GLL_POINTS = (-1.0, -math.sqrt(3.0 / 7.0), 0.0, math.sqrt(3.0 / 7.0), 1.0)
TIME_STEP = 0.2
STEP = TIME_STEP / SUBSTEPS
PAD_ROWS = 168


def slope_rows():
    points = GLL_POINTS
    rows = []
    for row_at in range(5):
        entries = []
        for col_at in range(5):
            if row_at == col_at:
                summed = 0.0
                for other_at in range(5):
                    if other_at != row_at:
                        summed += 1.0 / (points[row_at] - points[other_at])
                entries.append(summed)
            else:
                top_prod = 1.0
                low_prod = 1.0
                for other_at in range(5):
                    if other_at != row_at:
                        top_prod *= points[row_at] - points[other_at]
                    if other_at != col_at:
                        low_prod *= points[col_at] - points[other_at]
                entries.append(top_prod / low_prod / (points[row_at] - points[col_at]))
        rows.append(entries)
    return rows


def slope_operands():
    slopes = np.array(slope_rows(), dtype=np.float32)
    eye = np.eye(5, dtype=np.float32)
    along = [
        np.kron(np.kron(slopes, eye), eye),
        np.kron(np.kron(eye, slopes), eye),
        np.kron(np.kron(eye, eye), slopes),
    ]
    grad = np.zeros((LANES, 3 * LANES), np.float32)
    back = np.zeros((3 * LANES, LANES), np.float32)
    for i, matrix in enumerate(along):
        grad[:NODES, i * LANES : i * LANES + NODES] = matrix.T
        back[i * LANES : i * LANES + NODES, :NODES] = matrix

    def terms(whole):
        high = whole.astype(ml_dtypes.bfloat16)
        low = (whole - high.astype(np.float32)).astype(ml_dtypes.bfloat16)
        return np.concatenate([high, high, low], axis=0)

    return terms(grad), terms(back)


def split_terms(whole):
    high = whole.astype(jnp.bfloat16)
    low = (whole - high.astype(jnp.float32)).astype(jnp.bfloat16)
    return high, low


def lane_pick(values, index):
    return jnp.take_along_axis(values, index, axis=1, mode="promise_in_bounds")


def forces(shifted, jac, lam, mu, grad, back):
    count = shifted[0].shape[0]
    high, low = split_terms(jnp.concatenate(shifted, axis=0))
    slope = jnp.dot(
        jnp.concatenate([high, low, high], axis=1), grad, preferred_element_type=jnp.float32
    )
    strain = [
        [
            jac[i] * slope[c * count : (c + 1) * count, i * LANES : (i + 1) * LANES]
            for i in range(3)
        ]
        for c in range(3)
    ]
    traced = lam * (strain[0][0] + strain[1][1] + strain[2][2])
    rows = []
    for c in range(3):
        fluxes = []
        for i in range(3):
            stress = mu * (strain[c][i] + strain[i][c])
            if c == i:
                stress = stress + traced
            fluxes.append(jac[i] * stress)
        rows.append(jnp.concatenate(fluxes, axis=1))
    high, low = split_terms(jnp.concatenate(rows, axis=0))
    out = jnp.dot(
        jnp.concatenate([high, low, high], axis=1), back, preferred_element_type=jnp.float32
    )
    return [out[c * count : (c + 1) * count] for c in range(3)]


def inverse_rows(index, turned_ref, count, missing):
    turned_ref[...] = index.astype(jnp.float32).T
    target = lax.broadcasted_iota(jnp.int32, (LANES, LANES), 0).astype(jnp.float32)
    target = target.astype(jnp.bfloat16)
    found = jnp.full((LANES, LANES), missing, jnp.bfloat16)
    for k in range(count):
        row = jnp.broadcast_to(turned_ref[k : k + 1, :], (16, LANES)).astype(jnp.bfloat16)
        row = jnp.concatenate([row] * (LANES // 16), axis=0)
        found = jnp.where(row == target, jnp.full((LANES, LANES), k, jnp.bfloat16), found)
    return found.astype(jnp.float32).T.astype(jnp.int32)


def high_half(shape):
    return lax.broadcasted_iota(jnp.int32, shape, 1) >= LANES // 2


def fine_local(disp_ref, slots_ref, window_ref, statics, spread, grad, back):
    jac0, jac1, jac2, lam, mu, index, place = statics
    upper = high_half((1, LANES))
    for s in range(FCAP):
        e = slots_ref[s]
        first = lax.shift_right_logical(e, 1)
        second = lax.shift_right_logical(e + 1, 1)
        for c in range(3):
            window_ref[c, pl.ds(s, 1), :] = jnp.where(
                upper, disp_ref[c, pl.ds(first, 1), :], disp_ref[c, pl.ds(second, 1), :]
            )
    shifted = [lane_pick(window_ref[c], index) for c in range(3)]
    out = forces(shifted, (jac0, jac1, jac2), lam, mu, grad, back)
    slotted = jnp.concatenate([lane_pick(o, place) for o in out], axis=1)
    upper = lax.broadcasted_iota(jnp.int32, slotted.shape, 1) % LANES >= LANES // 2
    blank = jnp.zeros((LANES - FCAP, slotted.shape[1]), jnp.float32)
    both = jnp.concatenate(
        [jnp.where(upper, slotted, 0.0), blank, jnp.where(upper, 0.0, slotted), blank], axis=0
    )
    high, low = split_terms(both)
    return jnp.dot(spread, high, preferred_element_type=jnp.float32) + jnp.dot(
        spread, low, preferred_element_type=jnp.float32
    )


def send_pair(shared, picks, odd, staged_ref, outs):
    for c, values in enumerate(shared):
        staged_ref[c] = lane_pick(values, picks)
    for c in range(len(shared)):
        part = [staged_ref[c, GROUPS * p : GROUPS * (p + 1), :] for p in range(2)]
        put = pl.ds(c * GROUPS, GROUPS)
        outs[0][put, :] = jnp.where(odd, part[0], part[1])
        outs[1][put, :] = jnp.where(odd, part[1], part[0])


def received_pair(arrived, channels, places, odd, staged_ref):
    for c in range(channels):
        got = [a[c * GROUPS : (c + 1) * GROUPS, :] for a in arrived]
        staged_ref[c, 0:GROUPS, :] = jnp.where(odd, got[0][...], got[1][...])
        staged_ref[c, GROUPS : 2 * GROUPS, :] = jnp.where(odd, got[1][...], got[0][...])
    return [lane_pick(staged_ref[c], places) for c in range(channels)]


def odd_place(axis):
    return jnp.bitwise_and(lax.axis_index(axis), 1) == 1


def peer_maps(peer_ref, first, rows_ref):
    for p in range(2):
        for j in range(GROUPS):
            at = p * GROUPS + j
            rows_ref[at : at + 1, :] = peer_ref[
                first + p : first + p + 1, j * LANES : (j + 1) * LANES
            ] & (LANES - 1)


def element_rows(refs, low, count, pads, clear):
    jac_ref, lam_ref, mu_ref, dens_ref, conn_ref = refs
    value_ref, index_ref = pads
    if clear:
        value_ref[:, :, LANES - 8 :] = jnp.zeros_like(value_ref[:, :, LANES - 8 :])
        index_ref[:, LANES - 8 :] = jnp.zeros_like(index_ref[:, LANES - 8 :])
    sources = [jac_ref.at[0], jac_ref.at[1], jac_ref.at[2], lam_ref, mu_ref, dens_ref]
    for a, source in enumerate(sources):
        value_ref[a, 0:count, 0:NODES] = source[low : low + count, :]
    index_ref[0:count, 0:NODES] = conn_ref[low : low + count, :] & (LANES - 1)


def row_forces(low_row, part, disp_ref, disp_low, value_ref, index_ref, place_ref, first, grad, back, total_ref, total_low):
    upper = high_half((1, LANES))

    def paired(ref, *at):
        start = 2 * low_row - first
        return jnp.concatenate(
            [ref[(*at, pl.ds(start + odd, part, stride=2), slice(None))] for odd in range(2)],
            axis=0,
        )

    index, place = paired(index_ref), paired(place_ref)
    shifted = []
    at = low_row - disp_low
    for c in range(3):
        here = disp_ref[c, at : at + part, :]
        after = disp_ref[c, at + 1 : at + part + 1, :]
        shifted.append(
            lane_pick(jnp.concatenate([here, jnp.where(upper, here, after)], axis=0), index)
        )
    nodal = forces(
        shifted,
        [paired(value_ref, a) for a in range(3)],
        paired(value_ref, 3),
        paired(value_ref, 4),
        grad,
        back,
    )
    nodal.append(paired(value_ref, 5))
    at = low_row - total_low
    for c in range(4):
        spot = lane_pick(nodal[c], place)
        even, odd = spot[:part], spot[part:]
        total_ref[c, at : at + part, :] += even + jnp.where(upper, odd, 0.0)
        total_ref[c, at + 1 : at + part + 1, :] += jnp.where(upper, 0.0, odd)


def field_rows(source, low, count, out_ref):
    for j in range(count):
        row = (low + j) % ROWS
        for c in range(3):
            out_ref[c, j : j + 1, :] = source[
                c : c + 1, row * LANES : (row + 1) * LANES
            ]


EDGE = 8
HALF = 2 * GROUPS
WIDE = HALF + EDGE


def edge_kernel(
    axis,
    disp_in,
    jac_in,
    lam_in,
    mu_in,
    dens_in,
    conn_in,
    peer_in,
    grad_in,
    back_in,
    order_in,
    base_ref,
    spill_ref,
    sends0,
    sends1,
    value_ref,
    index_ref,
    place_ref,
    turned_ref,
    disp_ref,
    peer_rows_ref,
    staged_ref,
    total_ref,
    jac_ref,
    lam_ref,
    mu_ref,
    dens_ref,
    conn_ref,
    strip_ref,
    peer_ref,
    grad_ref,
    back_ref,
    sems,
):
    first = FIRST if axis == "dev" else FIRST + HALF
    low_row = first - EDGE
    count = 2 * WIDE
    part = pl.ds(2 * low_row, count)
    pairs = [
        (conn_in.at[part, :], conn_ref),
        (disp_in.at[:, pl.ds(low_row * LANES, WIDE * LANES)], strip_ref.at[:, 0 : WIDE * LANES]),
        (
            disp_in.at[:, pl.ds((low_row + WIDE) % ROWS * LANES, LANES)],
            strip_ref.at[:, WIDE * LANES : (WIDE + 1) * LANES],
        ),
        (grad_in, grad_ref),
        (jac_in.at[:, part, :], jac_ref),
        (lam_in.at[part, :], lam_ref),
        (mu_in.at[part, :], mu_ref),
        (dens_in.at[part, :], dens_ref),
        (back_in, back_ref),
        (peer_in, peer_ref),
    ]
    copies = [
        pltpu.make_async_copy(source, target, sems.at[i])
        for i, (source, target) in enumerate(pairs)
    ]
    for copy in copies:
        copy.start()
    index_ref[...] = jnp.zeros_like(index_ref)
    total_ref[...] = jnp.zeros_like(total_ref)
    for copy in copies:
        copy.wait()
    for j in range(WIDE + 1):
        for c in range(3):
            disp_ref[c, j : j + 1, :] = strip_ref[c : c + 1, j * LANES : (j + 1) * LANES]
    peer_maps(peer_ref, 0 if axis == "dev" else 2, peer_rows_ref)
    element_rows(
        (jac_ref, lam_ref, mu_ref, dens_ref, conn_ref), 0, count, (value_ref, index_ref), True
    )
    place_ref[...] = inverse_rows(index_ref[...], turned_ref, NODES, LANES - 1)
    row_forces(
        low_row,
        WIDE,
        disp_ref,
        low_row,
        value_ref,
        index_ref,
        place_ref,
        2 * low_row,
        grad_ref[...],
        back_ref[...],
        total_ref,
        low_row,
    )
    for c in range(4):
        base_ref[c] = total_ref[c, EDGE:WIDE, :]
        spill_ref[c] = total_ref[c, WIDE : WIDE + 8, :]
    send_pair(
        [base_ref[c] for c in range(4)],
        peer_rows_ref[...],
        odd_place(axis),
        staged_ref,
        (sends0, sends1),
    )


def inner_kernel(
    slots_ref,
    slot_row_ref,
    disp_in,
    veloc_in,
    jac_ref,
    lam_ref,
    mu_ref,
    dens_ref,
    conn_ref,
    peer_ref,
    spill_in,
    grad_ref,
    back_ref,
    veloc_ref,
    base_ref,
    fixed_ref,
    index_out,
    spread_ref,
    peer_index_ref,
    value_ref,
    index_ref,
    place_ref,
    turned_ref,
    disp_ref,
    peer_rows_ref,
    total_ref,
    spread_wide_ref,
):
    field_rows(disp_in, 0, FIRST + 1, disp_ref)
    field_rows(veloc_in, 0, ROWS, veloc_ref)
    index_ref[...] = jnp.zeros_like(index_ref)
    element_rows(
        (jac_ref, lam_ref, mu_ref, dens_ref, conn_ref), 0, ELEM, (value_ref, index_ref), True
    )
    value_ref[:, ELEM:, :] = jnp.zeros_like(value_ref[:, ELEM:, :])
    for s in range(FCAP):
        e = slots_ref[s]
        for a in range(5):
            fixed_ref[a, s : s + 1, :] = value_ref[a, pl.ds(e, 1), :]
        index_out[0, s : s + 1, :] = index_ref[pl.ds(e, 1), :]
    tail = ELEM // 2 - LANES
    place_ref[0:LANES, :] = inverse_rows(index_ref[0:LANES, :], turned_ref, NODES, LANES - 1)
    both = jnp.concatenate(
        [
            index_ref[LANES : LANES + tail, :],
            index_out[0],
            jnp.zeros((LANES - tail - FCAP, LANES), jnp.int32),
        ],
        axis=0,
    )
    found = inverse_rows(both, turned_ref, NODES, LANES - 1)
    place_ref[LANES : LANES + tail, :] = found[0:tail]
    index_out[1] = found[tail : tail + FCAP]
    for half in range(2):
        peer_maps(peer_ref, 2 * half, peer_rows_ref.at[pl.ds(half * HALF, HALF), :])
    peer_rows_ref[SHARED:, :] = jnp.zeros((LANES - SHARED, LANES), jnp.int32)
    peer_index_ref[0] = peer_rows_ref[0:SHARED, :]
    peer_index_ref[1] = inverse_rows(peer_rows_ref[...], turned_ref, LANES, 0)[0:SHARED]
    rows = lax.broadcasted_iota(jnp.int32, (ROWS, FCAP), 0)
    slot_row = slot_row_ref[...]
    second = lax.shift_right_logical(slot_row + 1, 1)
    second = jnp.where(second == ROWS, 0, second)
    spread_wide_ref[...] = jnp.zeros_like(spread_wide_ref)
    spread_wide_ref[:, 0:FCAP] = jnp.where(
        lax.shift_right_logical(slot_row, 1) == rows, 1.0, 0.0
    )
    spread_wide_ref[:, LANES : LANES + FCAP] = jnp.where(second == rows, 1.0, 0.0)
    spread_ref[...] = spread_wide_ref[...].astype(jnp.bfloat16)
    total_ref[...] = jnp.zeros_like(total_ref)
    for c in range(4):
        total_ref[c, 0:1, :] = spill_in[c, 0:1, :]
    for low_row in (0, HALF):
        row_forces(
            low_row,
            HALF,
            disp_ref,
            0,
            value_ref,
            index_ref,
            place_ref,
            0,
            grad_ref[...],
            back_ref[...],
            total_ref,
            0,
        )
    for c in range(4):
        base_ref[c] = total_ref[c, 0:FIRST, :]


def received_rows(arrived, channels, peer_index_ref, staged_ref):
    dev = received_pair(
        arrived[:2], channels, peer_index_ref[1, 0:HALF, :], odd_place("dev"), staged_ref
    )
    region = received_pair(
        arrived[2:], channels, peer_index_ref[1, HALF:, :], odd_place("region"), staged_ref
    )
    return [jnp.concatenate([d, r], axis=0) for d, r in zip(dev, region)]


def whole_base(c, inner_ref, dev_ref, region_ref):
    return jnp.concatenate([inner_ref[c], dev_ref[c], region_ref[c]], axis=0)


def middle_kernel(
    opening,
    slots_ref,
    moved_ref,
    veloc_ref,
    inner_ref,
    dev_ref,
    region_ref,
    summed_ref,
    inverse_ref,
    fixed_ref,
    index_ref,
    spread_ref,
    peer_index_ref,
    got0,
    got1,
    got2,
    got3,
    grad_ref,
    back_ref,
    moved_out,
    veloc_out,
    summed_out,
    *rest,
):
    if opening:
        inverse_out, sends0, sends1, sends2, sends3, window_ref, staged_ref = rest
    else:
        sends0, sends1, sends2, sends3, window_ref, staged_ref = rest
    placed = received_rows(
        (got0, got1, got2, got3), 4 if opening else 3, peer_index_ref, staged_ref
    )
    if opening:
        mass = whole_base(3, inner_ref, dev_ref, region_ref)
        inverse_out[0:FIRST, :] = 1.0 / mass[:FIRST]
        inverse_out[FIRST:, :] = 1.0 / (mass[FIRST:] + placed[3])
        inverse_mass = inverse_out[...]
    else:
        inverse_mass = inverse_ref[...]
    base = [whole_base(c, inner_ref, dev_ref, region_ref) for c in range(3)]
    for c in range(3):
        local = base[c] if opening else summed_ref[c]
        force = jnp.concatenate([local[:FIRST], local[FIRST:] + placed[c]], axis=0)
        v = veloc_ref[c] - STEP * (inverse_mass * force)
        moved = STEP * v if opening else moved_ref[c, 0:ROWS, :] + STEP * v
        moved_out[c, 0:ROWS, :] = moved
        moved_out[c, ROWS:PAD_ROWS, :] = jnp.broadcast_to(moved[0:1], (PAD_ROWS - ROWS, LANES))
        veloc_out[c] = v
    fine = fine_local(
        moved_out,
        slots_ref,
        window_ref,
        [fixed_ref[a] for a in range(5)] + [index_ref[a] for a in range(2)],
        spread_ref[...],
        grad_ref[...],
        back_ref[...],
    )
    for c in range(3):
        summed_out[c] = base[c] + fine[:, c * LANES : (c + 1) * LANES]
    for axis, at, outs in (("dev", 0, (sends0, sends1)), ("region", HALF, (sends2, sends3))):
        send_pair(
            [summed_out[c, FIRST + at : FIRST + at + HALF, :] for c in range(3)],
            peer_index_ref[0, at : at + HALF, :],
            odd_place(axis),
            staged_ref,
            outs,
        )


def last_kernel(
    disp_in,
    moved_ref,
    veloc_ref,
    summed_ref,
    inverse_ref,
    peer_index_ref,
    got0,
    got1,
    got2,
    got3,
    disp_out,
    veloc_out,
    staged_ref,
    rows_ref,
):
    placed = received_rows((got0, got1, got2, got3), 3, peer_index_ref, staged_ref)
    for c in range(3):
        force = jnp.concatenate(
            [summed_ref[c, :FIRST, :], summed_ref[c, FIRST:, :] + placed[c]], axis=0
        )
        v = veloc_ref[c] - STEP * (inverse_ref[...] * force)
        rows_ref[0, c] = moved_ref[c, 0:ROWS, :] + STEP * v
        rows_ref[1, c] = v
    for j in range(ROWS):
        cols = slice(j * LANES, (j + 1) * LANES)
        for c in range(3):
            disp_out[c : c + 1, cols] = disp_in[c : c + 1, cols] + rows_ref[0, c, j : j + 1, :]
            veloc_out[c : c + 1, cols] = rows_ref[1, c, j : j + 1, :]


def swap_pairs(count, colour):
    pairs = []
    for low in range(colour, count, 2):
        high = (low + 1) % count
        pairs += [(low, high), (high, low)]
    return pairs


def swap_all(sends, axis):
    return [
        lax.ppermute(sent, axis, swap_pairs(lax.axis_size(axis), colour))
        for colour, sent in enumerate(sends)
    ]


def shape(dims, kind=jnp.float32):
    return jax.ShapeDtypeStruct(dims, kind)


def scratch(*dims, kind=jnp.float32):
    return pltpu.VMEM(dims, kind)


PARAMS = pltpu.CompilerParams(vmem_limit_bytes=48 * 1024 * 1024)
ALONE = pltpu.CompilerParams(vmem_limit_bytes=62 * 1024 * 1024)


def body(
    disp_start,
    veloc_start,
    jacobian,
    lame_lambda,
    lame_mu,
    density,
    connect,
    fine_slots,
    peer_nodes,
):
    grad_np, back_np = slope_operands()
    grad, back = jnp.asarray(grad_np), jnp.asarray(back_np)
    scalar = pl.BlockSpec(memory_space=pltpu.SMEM)
    vector = pl.BlockSpec(memory_space=pltpu.VMEM)
    field = shape((3, ROWS, LANES))
    padded = shape((3, PAD_ROWS, LANES))
    elements = (
        jnp.transpose(jacobian, (0, 2, 1)),
        lame_lambda.T,
        lame_mu.T,
        density.T,
        connect.T,
    )

    def sends(channels, count):
        return [shape((channels * GROUPS, LANES))] * count

    got, bases = [], []
    raw = pl.BlockSpec(memory_space=pltpu.HBM)
    order = peer_nodes
    count = 2 * WIDE
    for axis in ("dev", "region"):
        base, spill, send0, send1 = pl.pallas_call(
            functools.partial(edge_kernel, axis),
            in_specs=[raw] * 9 + [pl.BlockSpec(memory_space=pl.ANY)],
            out_shape=[shape((4, HALF, LANES)), shape((4, 8, LANES))] + sends(4, 2),
            out_specs=[vector] * 4,
            scratch_shapes=[
                scratch(6, LANES, LANES),
                scratch(LANES, LANES, kind=jnp.int32),
                scratch(LANES, LANES, kind=jnp.int32),
                scratch(LANES, LANES),
                scratch(3, WIDE + 8, LANES),
                scratch(HALF, LANES, kind=jnp.int32),
                scratch(4, HALF, LANES),
                scratch(4, WIDE + 8, LANES),
                scratch(3, count, NODES),
                scratch(count, NODES),
                scratch(count, NODES),
                scratch(count, NODES),
                scratch(count, NODES, kind=jnp.int32),
                scratch(3, (WIDE + 1) * LANES),
                scratch(4, GROUPS * LANES, kind=jnp.int32),
                scratch(*grad_np.shape, kind=jnp.bfloat16),
                scratch(*back_np.shape, kind=jnp.bfloat16),
                pltpu.SemaphoreType.DMA((10,)),
            ],
            compiler_params=PARAMS,
            name="edge_" + axis,
        )(*[pltpu.with_memory_space_constraint(x, pltpu.HBM) for x in (disp_start, *elements, peer_nodes, grad, back)], order)
        order = spill
        got += swap_all((send0, send1), axis)
        bases.append(base)
    veloc, inner, fixed, index, spread, peer_index = pl.pallas_call(
        inner_kernel,
        in_specs=[scalar] + [vector] * 12,
        out_shape=[
            field,
            shape((4, FIRST, LANES)),
            shape((5, FCAP, LANES)),
            shape((2, FCAP, LANES), jnp.int32),
            shape((ROWS, 2 * LANES), jnp.bfloat16),
            shape((2, SHARED, LANES), jnp.int32),
        ],
        out_specs=[vector] * 6,
        scratch_shapes=[
            scratch(6, ELEM + 8, LANES),
            scratch(ELEM + 8, LANES, kind=jnp.int32),
            scratch(ELEM // 2, LANES, kind=jnp.int32),
            scratch(LANES, LANES),
            scratch(3, FIRST + 8, LANES),
            scratch(LANES, LANES, kind=jnp.int32),
            scratch(4, FIRST + 8, LANES),
            scratch(ROWS, 2 * LANES),
        ],
        compiler_params=PARAMS,
        name="inner",
    )(
        fine_slots,
        fine_slots.reshape(1, FCAP),
        disp_start,
        veloc_start,
        *elements,
        peer_nodes,
        spill,
        grad,
        back,
    )
    inverse_mass, moved, summed = peer_index, peer_index, peer_index
    for substep in range(SUBSTEPS - 1):
        opening = substep == 0
        extra = [shape((ROWS, LANES))] if opening else []
        outs = pl.pallas_call(
            functools.partial(middle_kernel, opening),
            in_specs=[scalar] + [vector] * 17,
            out_shape=[padded, field, field] + extra + sends(3, 4),
            out_specs=[vector] * (7 + len(extra)),
            scratch_shapes=[
                scratch(3, FCAP, LANES),
                scratch(4, HALF, LANES),
            ],
            compiler_params=PARAMS,
            name="middle",
        )(
            fine_slots,
            moved,
            veloc,
            inner,
            *bases,
            summed,
            inverse_mass,
            fixed,
            index,
            spread,
            peer_index,
            *got,
            grad,
            back,
        )
        moved, veloc, summed = outs[:3]
        if opening:
            inverse_mass = outs[3]
        got = swap_all(outs[-4:-2], "dev") + swap_all(outs[-2:], "region")
    return pl.pallas_call(
        last_kernel,
        in_specs=[vector] * 10,
        out_shape=[shape((3, NLOC)), shape((3, NLOC))],
        out_specs=[vector] * 2,
        scratch_shapes=[
            scratch(4, HALF, LANES),
            scratch(2, 3, ROWS, LANES),
        ],
        compiler_params=PARAMS,
        name="last",
    )(disp_start, moved, veloc, summed, inverse_mass, peer_index, *got)


def solution(mesh):
    in_specs = (
        P(None, ("region", "dev")),
        P(None, ("region", "dev")),
        P(None, None, ("region", "dev")),
        P(None, ("region", "dev")),
        P(None, ("region", "dev")),
        P(None, ("region", "dev")),
        P(None, ("region", "dev")),
        P(("region", "dev")),
        P(None, ("region", "dev")),
    )
    out_specs = (P(None, ("region", "dev")), P(None, ("region", "dev")))
    return jax.shard_map(body, mesh=mesh, in_specs=in_specs, out_specs=out_specs, check_vma=False)
```

```python
import functools
import math

import jax
import jax.numpy as jnp
import ml_dtypes
import numpy as np
from jax import lax
from jax.experimental import pallas as pl
from jax.experimental.pallas import tpu as pltpu
from jax.sharding import PartitionSpec as P

NODES = 125
ELEM = 320
NLOC = 20480
FCAP = 80
LANES = 128
ROWS = NLOC // LANES
FIRST = ROWS // 2
GROUPS = 20
SHARED = 4 * GROUPS
SUBSTEPS = 4
GLL_POINTS = (-1.0, -math.sqrt(3.0 / 7.0), 0.0, math.sqrt(3.0 / 7.0), 1.0)
TIME_STEP = 0.2
STEP = TIME_STEP / SUBSTEPS
PAD_ROWS = 168


def slope_rows():
    points = GLL_POINTS
    rows = []
    for row_at in range(5):
        entries = []
        for col_at in range(5):
            if row_at == col_at:
                summed = 0.0
                for other_at in range(5):
                    if other_at != row_at:
                        summed += 1.0 / (points[row_at] - points[other_at])
                entries.append(summed)
            else:
                top_prod = 1.0
                low_prod = 1.0
                for other_at in range(5):
                    if other_at != row_at:
                        top_prod *= points[row_at] - points[other_at]
                    if other_at != col_at:
                        low_prod *= points[col_at] - points[other_at]
                entries.append(top_prod / low_prod / (points[row_at] - points[col_at]))
        rows.append(entries)
    return rows


def slope_operands():
    slopes = np.array(slope_rows(), dtype=np.float32)
    eye = np.eye(5, dtype=np.float32)
    along = [
        np.kron(np.kron(slopes, eye), eye),
        np.kron(np.kron(eye, slopes), eye),
        np.kron(np.kron(eye, eye), slopes),
    ]
    grad = np.zeros((LANES, 3 * LANES), np.float32)
    back = np.zeros((3 * LANES, LANES), np.float32)
    for i, matrix in enumerate(along):
        grad[:NODES, i * LANES : i * LANES + NODES] = matrix.T
        back[i * LANES : i * LANES + NODES, :NODES] = matrix

    def terms(whole):
        high = whole.astype(ml_dtypes.bfloat16)
        low = (whole - high.astype(np.float32)).astype(ml_dtypes.bfloat16)
        return np.concatenate([high, high, low], axis=0)

    return terms(grad), terms(back)


def split_terms(whole):
    high = whole.astype(jnp.bfloat16)
    low = (whole - high.astype(jnp.float32)).astype(jnp.bfloat16)
    return high, low


def lane_pick(values, index):
    return jnp.take_along_axis(values, index, axis=1, mode="promise_in_bounds")


def forces(shifted, jac, lam, mu, grad, back):
    count = shifted[0].shape[0]
    high, low = split_terms(jnp.concatenate(shifted, axis=0))
    slope = jnp.dot(
        jnp.concatenate([high, low, high], axis=1), grad, preferred_element_type=jnp.float32
    )
    strain = [
        [
            jac[i] * slope[c * count : (c + 1) * count, i * LANES : (i + 1) * LANES]
            for i in range(3)
        ]
        for c in range(3)
    ]
    traced = lam * (strain[0][0] + strain[1][1] + strain[2][2])
    rows = []
    for c in range(3):
        fluxes = []
        for i in range(3):
            stress = mu * (strain[c][i] + strain[i][c])
            if c == i:
                stress = stress + traced
            fluxes.append(jac[i] * stress)
        rows.append(jnp.concatenate(fluxes, axis=1))
    high, low = split_terms(jnp.concatenate(rows, axis=0))
    out = jnp.dot(
        jnp.concatenate([high, low, high], axis=1), back, preferred_element_type=jnp.float32
    )
    return [out[c * count : (c + 1) * count] for c in range(3)]


def inverse_rows(index, turned_ref, count, missing):
    turned_ref[...] = index.astype(jnp.float32).T
    target = lax.broadcasted_iota(jnp.int32, (LANES, LANES), 0).astype(jnp.float32)
    target = target.astype(jnp.bfloat16)
    found = jnp.full((LANES, LANES), missing, jnp.bfloat16)
    for k in range(count):
        row = jnp.broadcast_to(turned_ref[k : k + 1, :], (16, LANES)).astype(jnp.bfloat16)
        row = jnp.concatenate([row] * (LANES // 16), axis=0)
        found = jnp.where(row == target, jnp.full((LANES, LANES), k, jnp.bfloat16), found)
    return found.astype(jnp.float32).T.astype(jnp.int32)


def high_half(shape):
    return lax.broadcasted_iota(jnp.int32, shape, 1) >= LANES // 2


def fine_local(disp_ref, slots_ref, window_ref, statics, spread, grad, back):
    jac0, jac1, jac2, lam, mu, index, place = statics
    upper = high_half((1, LANES))
    for s in range(FCAP):
        e = slots_ref[s]
        first = lax.shift_right_logical(e, 1)
        second = lax.shift_right_logical(e + 1, 1)
        for c in range(3):
            window_ref[c, pl.ds(s, 1), :] = jnp.where(
                upper, disp_ref[c, pl.ds(first, 1), :], disp_ref[c, pl.ds(second, 1), :]
            )
    shifted = [lane_pick(window_ref[c], index) for c in range(3)]
    out = forces(shifted, (jac0, jac1, jac2), lam, mu, grad, back)
    slotted = jnp.concatenate([lane_pick(o, place) for o in out], axis=1)
    upper = lax.broadcasted_iota(jnp.int32, slotted.shape, 1) % LANES >= LANES // 2
    blank = jnp.zeros((LANES - FCAP, slotted.shape[1]), jnp.float32)
    both = jnp.concatenate(
        [jnp.where(upper, slotted, 0.0), blank, jnp.where(upper, 0.0, slotted), blank], axis=0
    )
    high, low = split_terms(both)
    return jnp.dot(spread, high, preferred_element_type=jnp.float32) + jnp.dot(
        spread, low, preferred_element_type=jnp.float32
    )


def send_pair(shared, picks, odd, staged_ref, outs):
    for c, values in enumerate(shared):
        staged_ref[c] = lane_pick(values, picks)
    for c in range(len(shared)):
        part = [staged_ref[c, GROUPS * p : GROUPS * (p + 1), :] for p in range(2)]
        put = pl.ds(c * GROUPS, GROUPS)
        outs[0][put, :] = jnp.where(odd, part[0], part[1])
        outs[1][put, :] = jnp.where(odd, part[1], part[0])


def received_pair(arrived, channels, places, odd, staged_ref):
    for c in range(channels):
        got = [a[c * GROUPS : (c + 1) * GROUPS, :] for a in arrived]
        staged_ref[c, 0:GROUPS, :] = jnp.where(odd, got[0][...], got[1][...])
        staged_ref[c, GROUPS : 2 * GROUPS, :] = jnp.where(odd, got[1][...], got[0][...])
    return [lane_pick(staged_ref[c], places) for c in range(channels)]


def odd_place(axis):
    return jnp.bitwise_and(lax.axis_index(axis), 1) == 1


def peer_maps(peer_ref, first, rows_ref):
    for p in range(2):
        for j in range(GROUPS):
            at = p * GROUPS + j
            rows_ref[at : at + 1, :] = peer_ref[
                first + p : first + p + 1, j * LANES : (j + 1) * LANES
            ] & (LANES - 1)


def index_rows(conn_ref, low, count, index_ref):
    index_ref[...] = jnp.zeros_like(index_ref)
    index_ref[0:count, 0:NODES] = conn_ref[low : low + count, :] & (LANES - 1)


def value_rows(refs, low, count, value_ref):
    jac_ref, lam_ref, mu_ref, dens_ref = refs
    value_ref[:, :, LANES - 8 :] = jnp.zeros_like(value_ref[:, :, LANES - 8 :])
    sources = [jac_ref.at[0], jac_ref.at[1], jac_ref.at[2], lam_ref, mu_ref, dens_ref]
    for a, source in enumerate(sources):
        value_ref[a, 0:count, 0:NODES] = source[low : low + count, :]


def row_forces(low_row, part, disp_ref, disp_low, value_ref, index_ref, place_ref, first, grad, back, total_ref, total_low):
    upper = high_half((1, LANES))

    def paired(ref, *at):
        start = 2 * low_row - first
        return jnp.concatenate(
            [ref[(*at, pl.ds(start + odd, part, stride=2), slice(None))] for odd in range(2)],
            axis=0,
        )

    index, place = paired(index_ref), paired(place_ref)
    shifted = []
    at = low_row - disp_low
    for c in range(3):
        here = disp_ref[c, at : at + part, :]
        after = disp_ref[c, at + 1 : at + part + 1, :]
        shifted.append(
            lane_pick(jnp.concatenate([here, jnp.where(upper, here, after)], axis=0), index)
        )
    nodal = forces(
        shifted,
        [paired(value_ref, a) for a in range(3)],
        paired(value_ref, 3),
        paired(value_ref, 4),
        grad,
        back,
    )
    nodal.append(paired(value_ref, 5))
    at = low_row - total_low
    for c in range(4):
        spot = lane_pick(nodal[c], place)
        even, odd = spot[:part], spot[part:]
        total_ref[c, at : at + part, :] += even + jnp.where(upper, odd, 0.0)
        total_ref[c, at + 1 : at + part + 1, :] += jnp.where(upper, 0.0, odd)


def field_rows(source, low, count, out_ref):
    for j in range(count):
        row = (low + j) % ROWS
        for c in range(3):
            out_ref[c, j : j + 1, :] = source[
                c : c + 1, row * LANES : (row + 1) * LANES
            ]


EDGE = 8
HALF = 2 * GROUPS
WIDE = HALF + EDGE


def edge_part(axis, ready, sources, outs, scratches):
    disp_in, jac_ref, lam_ref, mu_ref, dens_ref, conn_ref, peer_ref, grad_ref, back_ref = sources
    base_ref, spill_ref, sends0, sends1 = outs
    (
        value_ref,
        index_ref,
        place_ref,
        turned_ref,
        disp_ref,
        peer_rows_ref,
        staged_ref,
        total_ref,
    ) = scratches
    first = FIRST if axis == "dev" else FIRST + HALF
    low_row = first - EDGE
    total_ref[...] = jnp.zeros_like(total_ref)
    ready(0)
    index_rows(conn_ref, 2 * low_row, 2 * WIDE, index_ref)
    place_ref[...] = inverse_rows(index_ref[...], turned_ref, NODES, LANES - 1)
    ready(1)
    field_rows(disp_in, low_row, WIDE + 1, disp_ref)
    peer_maps(peer_ref, 0 if axis == "dev" else 2, peer_rows_ref)
    ready(2)
    value_rows((jac_ref, lam_ref, mu_ref, dens_ref), 2 * low_row, 2 * WIDE, value_ref)
    row_forces(
        low_row,
        WIDE,
        disp_ref,
        low_row,
        value_ref,
        index_ref,
        place_ref,
        2 * low_row,
        grad_ref[...],
        back_ref[...],
        total_ref,
        low_row,
    )
    for c in range(4):
        base_ref[c] = total_ref[c, EDGE:WIDE, :]
        spill_ref[c] = total_ref[c, WIDE : WIDE + 8, :]
    send_pair(
        [base_ref[c] for c in range(4)],
        peer_rows_ref[...],
        odd_place(axis),
        staged_ref,
        (sends0, sends1),
    )


def dev_edge_kernel(*refs):
    raw, kept, outs, scratches = refs[:10], refs[10:20], refs[20:24], refs[24:32]
    sems = refs[32]
    disp_in, veloc_in, jac_in, lam_in, mu_in, dens_in, conn_in, peer_in, grad_in, back_in = raw
    disp, veloc, jac, lam, mu, dens, conn, peer, grad, back = kept
    low = 2 * (FIRST - EDGE)
    mine, lower, upper = pl.ds(low, 2 * WIDE), pl.ds(0, low), pl.ds(low + 2 * WIDE, ELEM - low - 2 * WIDE)
    steps = [
        [(conn_in.at[mine, :], conn.at[mine, :])],
        [(disp_in, disp), (peer_in, peer)],
        [(jac_in.at[:, mine, :], jac.at[:, mine, :]), (grad_in, grad)]
        + [(x.at[mine, :], y.at[mine, :]) for x, y in ((lam_in, lam), (mu_in, mu), (dens_in, dens))]
        + [(back_in, back)],
        [(veloc_in, veloc)]
        + [(jac_in.at[:, part, :], jac.at[:, part, :]) for part in (upper, lower)]
        + [
            (x.at[part, :], y.at[part, :])
            for part in (upper, lower)
            for x, y in ((lam_in, lam), (mu_in, mu), (dens_in, dens), (conn_in, conn))
        ],
    ]
    copies, count = [], 0
    for step in steps:
        group = []
        for source, target in step:
            group.append(pltpu.make_async_copy(source, target, sems.at[count]))
            count += 1
        copies.append(group)
    for group in copies:
        for copy in group:
            copy.start()

    def ready(step):
        for copy in copies[step]:
            copy.wait()

    edge_part("dev", ready, (disp,) + tuple(kept[2:]), outs, scratches)
    ready(3)


def region_edge_kernel(*refs):
    edge_part("region", lambda step: None, refs[:9], refs[10:14], refs[14:22])


def inner_kernel(
    slots_ref,
    slot_row_ref,
    disp_in,
    veloc_in,
    jac_ref,
    lam_ref,
    mu_ref,
    dens_ref,
    conn_ref,
    peer_ref,
    spill_in,
    grad_ref,
    back_ref,
    veloc_ref,
    base_ref,
    fixed_ref,
    index_out,
    spread_ref,
    peer_index_ref,
    value_ref,
    index_ref,
    place_ref,
    turned_ref,
    disp_ref,
    peer_rows_ref,
    total_ref,
    spread_wide_ref,
):
    field_rows(disp_in, 0, FIRST + 1, disp_ref)
    field_rows(veloc_in, 0, ROWS, veloc_ref)
    index_rows(conn_ref, 0, ELEM, index_ref)
    value_rows((jac_ref, lam_ref, mu_ref, dens_ref), 0, ELEM, value_ref)
    value_ref[:, ELEM:, :] = jnp.zeros_like(value_ref[:, ELEM:, :])
    for s in range(FCAP):
        e = slots_ref[s]
        for a in range(5):
            fixed_ref[a, s : s + 1, :] = value_ref[a, pl.ds(e, 1), :]
        index_out[0, s : s + 1, :] = index_ref[pl.ds(e, 1), :]
    tail = ELEM // 2 - LANES
    place_ref[0:LANES, :] = inverse_rows(index_ref[0:LANES, :], turned_ref, NODES, LANES - 1)
    both = jnp.concatenate(
        [
            index_ref[LANES : LANES + tail, :],
            index_out[0],
            jnp.zeros((LANES - tail - FCAP, LANES), jnp.int32),
        ],
        axis=0,
    )
    found = inverse_rows(both, turned_ref, NODES, LANES - 1)
    place_ref[LANES : LANES + tail, :] = found[0:tail]
    index_out[1] = found[tail : tail + FCAP]
    for half in range(2):
        peer_maps(peer_ref, 2 * half, peer_rows_ref.at[pl.ds(half * HALF, HALF), :])
    peer_rows_ref[SHARED:, :] = jnp.zeros((LANES - SHARED, LANES), jnp.int32)
    peer_index_ref[0] = peer_rows_ref[0:SHARED, :]
    peer_index_ref[1] = inverse_rows(peer_rows_ref[...], turned_ref, LANES, 0)[0:SHARED]
    rows = lax.broadcasted_iota(jnp.int32, (ROWS, FCAP), 0)
    slot_row = slot_row_ref[...]
    second = lax.shift_right_logical(slot_row + 1, 1)
    second = jnp.where(second == ROWS, 0, second)
    spread_wide_ref[...] = jnp.zeros_like(spread_wide_ref)
    spread_wide_ref[:, 0:FCAP] = jnp.where(
        lax.shift_right_logical(slot_row, 1) == rows, 1.0, 0.0
    )
    spread_wide_ref[:, LANES : LANES + FCAP] = jnp.where(second == rows, 1.0, 0.0)
    spread_ref[...] = spread_wide_ref[...].astype(jnp.bfloat16)
    total_ref[...] = jnp.zeros_like(total_ref)
    for c in range(4):
        total_ref[c, 0:1, :] = spill_in[c, 0:1, :]
    for low_row in (0, HALF):
        row_forces(
            low_row,
            HALF,
            disp_ref,
            0,
            value_ref,
            index_ref,
            place_ref,
            0,
            grad_ref[...],
            back_ref[...],
            total_ref,
            0,
        )
    for c in range(4):
        base_ref[c] = total_ref[c, 0:FIRST, :]


def received_rows(arrived, channels, peer_index_ref, staged_ref):
    dev = received_pair(
        arrived[:2], channels, peer_index_ref[1, 0:HALF, :], odd_place("dev"), staged_ref
    )
    region = received_pair(
        arrived[2:], channels, peer_index_ref[1, HALF:, :], odd_place("region"), staged_ref
    )
    return [jnp.concatenate([d, r], axis=0) for d, r in zip(dev, region)]


def whole_base(c, inner_ref, dev_ref, region_ref):
    return jnp.concatenate([inner_ref[c], dev_ref[c], region_ref[c]], axis=0)


def middle_kernel(
    opening,
    slots_ref,
    moved_ref,
    veloc_ref,
    inner_ref,
    dev_ref,
    region_ref,
    summed_ref,
    inverse_ref,
    fixed_ref,
    index_ref,
    spread_ref,
    peer_index_ref,
    got0,
    got1,
    got2,
    got3,
    grad_ref,
    back_ref,
    moved_out,
    veloc_out,
    summed_out,
    *rest,
):
    if opening:
        inverse_out, sends0, sends1, sends2, sends3, window_ref, staged_ref = rest
    else:
        sends0, sends1, sends2, sends3, window_ref, staged_ref = rest
    placed = received_rows(
        (got0, got1, got2, got3), 4 if opening else 3, peer_index_ref, staged_ref
    )
    if opening:
        mass = whole_base(3, inner_ref, dev_ref, region_ref)
        inverse_out[0:FIRST, :] = 1.0 / mass[:FIRST]
        inverse_out[FIRST:, :] = 1.0 / (mass[FIRST:] + placed[3])
        inverse_mass = inverse_out[...]
    else:
        inverse_mass = inverse_ref[...]
    base = [whole_base(c, inner_ref, dev_ref, region_ref) for c in range(3)]
    for c in range(3):
        local = base[c] if opening else summed_ref[c]
        force = jnp.concatenate([local[:FIRST], local[FIRST:] + placed[c]], axis=0)
        v = veloc_ref[c] - STEP * (inverse_mass * force)
        moved = STEP * v if opening else moved_ref[c, 0:ROWS, :] + STEP * v
        moved_out[c, 0:ROWS, :] = moved
        moved_out[c, ROWS:PAD_ROWS, :] = jnp.broadcast_to(moved[0:1], (PAD_ROWS - ROWS, LANES))
        veloc_out[c] = v
    fine = fine_local(
        moved_out,
        slots_ref,
        window_ref,
        [fixed_ref[a] for a in range(5)] + [index_ref[a] for a in range(2)],
        spread_ref[...],
        grad_ref[...],
        back_ref[...],
    )
    for c in range(3):
        summed_out[c] = base[c] + fine[:, c * LANES : (c + 1) * LANES]
    for axis, at, outs in (("dev", 0, (sends0, sends1)), ("region", HALF, (sends2, sends3))):
        send_pair(
            [summed_out[c, FIRST + at : FIRST + at + HALF, :] for c in range(3)],
            peer_index_ref[0, at : at + HALF, :],
            odd_place(axis),
            staged_ref,
            outs,
        )


def last_rows(low, count, force, refs, outs, scratches):
    disp_in, moved_ref, veloc_ref, inverse_ref = refs
    rows_ref, lines_ref, sems = scratches
    part = pl.ds(low, count)
    for c in range(3):
        v = veloc_ref[c, part, :] - STEP * (inverse_ref[part, :] * force[c])
        rows_ref[0, c] = moved_ref[c, part, :] + STEP * v
        rows_ref[1, c] = v
    copies = []
    for which in (1, 0):
        for j in range(count):
            cols = slice(j * LANES, (j + 1) * LANES)
            whole = slice((low + j) * LANES, (low + j + 1) * LANES)
            for c in range(3):
                row = rows_ref[which, c, j : j + 1, :]
                if which == 0:
                    row = disp_in[c : c + 1, whole] + row
                lines_ref[which, c : c + 1, cols] = row
        copy = pltpu.make_async_copy(
            lines_ref.at[which],
            outs[which].at[:, pl.ds(low * LANES, count * LANES)],
            sems.at[which],
        )
        copy.start()
        copies.append(copy)
    for copy in copies:
        copy.wait()


def inner_last_kernel(
    disp_in, moved_ref, veloc_ref, summed_ref, inverse_ref, disp_out, veloc_out, *scratches
):
    last_rows(
        0,
        FIRST,
        [summed_ref[c, :FIRST, :] for c in range(3)],
        (disp_in, moved_ref, veloc_ref, inverse_ref),
        (disp_out, veloc_out),
        scratches,
    )


def edge_last_kernel(
    disp_in,
    moved_ref,
    veloc_ref,
    summed_ref,
    inverse_ref,
    peer_index_ref,
    got0,
    got1,
    got2,
    got3,
    disp_half,
    veloc_half,
    disp_out,
    veloc_out,
    staged_ref,
    *scratches,
):
    placed = received_rows((got0, got1, got2, got3), 3, peer_index_ref, staged_ref)
    last_rows(
        FIRST,
        FIRST,
        [summed_ref[c, FIRST:, :] + placed[c] for c in range(3)],
        (disp_in, moved_ref, veloc_ref, inverse_ref),
        (disp_out, veloc_out),
        scratches,
    )


def swap_pairs(count, colour):
    pairs = []
    for low in range(colour, count, 2):
        high = (low + 1) % count
        pairs += [(low, high), (high, low)]
    return pairs


def swap_all(sends, axis):
    return [
        lax.ppermute(sent, axis, swap_pairs(lax.axis_size(axis), colour))
        for colour, sent in enumerate(sends)
    ]


def shape(dims, kind=jnp.float32):
    return jax.ShapeDtypeStruct(dims, kind)


def scratch(*dims, kind=jnp.float32):
    return pltpu.VMEM(dims, kind)


PARAMS = pltpu.CompilerParams(vmem_limit_bytes=48 * 1024 * 1024)


def body(
    disp_start,
    veloc_start,
    jacobian,
    lame_lambda,
    lame_mu,
    density,
    connect,
    fine_slots,
    peer_nodes,
):
    grad_np, back_np = slope_operands()
    grad, back = jnp.asarray(grad_np), jnp.asarray(back_np)
    scalar = pl.BlockSpec(memory_space=pltpu.SMEM)
    vector = pl.BlockSpec(memory_space=pltpu.VMEM)
    field = shape((3, ROWS, LANES))
    padded = shape((3, PAD_ROWS, LANES))
    elements = (
        jnp.transpose(jacobian, (0, 2, 1)),
        lame_lambda.T,
        lame_mu.T,
        density.T,
        connect.T,
    )

    def sends(channels, count):
        return [shape((channels * GROUPS, LANES))] * count

    got, bases = [], []
    raw = pl.BlockSpec(memory_space=pltpu.HBM)
    arguments = (disp_start, veloc_start, *elements, peer_nodes, grad, back)
    edge_outs = [shape((4, HALF, LANES)), shape((4, 8, LANES))] + sends(4, 2)
    edge_scratch = [
        scratch(6, LANES, LANES),
        scratch(LANES, LANES, kind=jnp.int32),
        scratch(LANES, LANES, kind=jnp.int32),
        scratch(LANES, LANES),
        scratch(3, WIDE + 8, LANES),
        scratch(HALF, LANES, kind=jnp.int32),
        scratch(4, HALF, LANES),
        scratch(4, WIDE + 8, LANES),
    ]
    outs = pl.pallas_call(
        dev_edge_kernel,
        in_specs=[raw] * 10,
        out_shape=[shape(x.shape, x.dtype) for x in arguments] + edge_outs,
        out_specs=[vector] * 14,
        scratch_shapes=edge_scratch + [pltpu.SemaphoreType.DMA((20,))],
        compiler_params=PARAMS,
        name="edge_dev",
    )(*[pltpu.with_memory_space_constraint(x, pltpu.HBM) for x in arguments])
    disp_near, veloc_near, *near = outs[:10]
    base, order, send0, send1 = outs[10:]
    bases.append(base)
    got += swap_all((send0, send1), "dev")
    base, spill, send0, send1 = pl.pallas_call(
        region_edge_kernel,
        in_specs=[vector] * 10,
        out_shape=edge_outs,
        out_specs=[vector] * 4,
        scratch_shapes=edge_scratch,
        compiler_params=PARAMS,
        name="edge_region",
    )(disp_near, *near, order)
    bases.append(base)
    got += swap_all((send0, send1), "region")
    veloc, inner, fixed, index, spread, peer_index = pl.pallas_call(
        inner_kernel,
        in_specs=[scalar] + [vector] * 12,
        out_shape=[
            field,
            shape((4, FIRST, LANES)),
            shape((5, FCAP, LANES)),
            shape((2, FCAP, LANES), jnp.int32),
            shape((ROWS, 2 * LANES), jnp.bfloat16),
            shape((2, SHARED, LANES), jnp.int32),
        ],
        out_specs=[vector] * 6,
        scratch_shapes=[
            scratch(6, ELEM + 8, LANES),
            scratch(ELEM + 8, LANES, kind=jnp.int32),
            scratch(ELEM // 2, LANES, kind=jnp.int32),
            scratch(LANES, LANES),
            scratch(3, FIRST + 8, LANES),
            scratch(LANES, LANES, kind=jnp.int32),
            scratch(4, FIRST + 8, LANES),
            scratch(ROWS, 2 * LANES),
        ],
        compiler_params=PARAMS,
        name="inner",
    )(
        fine_slots,
        fine_slots.reshape(1, FCAP),
        disp_near,
        veloc_near,
        *near[:6],
        spill,
        *near[6:],
    )
    inverse_mass, moved, summed = peer_index, peer_index, peer_index
    for substep in range(SUBSTEPS - 1):
        opening = substep == 0
        extra = [shape((ROWS, LANES))] if opening else []
        outs = pl.pallas_call(
            functools.partial(middle_kernel, opening),
            in_specs=[scalar] + [vector] * 17,
            out_shape=[padded, field, field] + extra + sends(3, 4),
            out_specs=[vector] * (7 + len(extra)),
            scratch_shapes=[
                scratch(3, FCAP, LANES),
                scratch(4, HALF, LANES),
            ],
            compiler_params=PARAMS,
            name="middle",
        )(
            fine_slots,
            moved,
            veloc,
            inner,
            *bases,
            summed,
            inverse_mass,
            fixed,
            index,
            spread,
            peer_index,
            *got,
            grad,
            back,
        )
        moved, veloc, summed = outs[:3]
        if opening:
            inverse_mass = outs[3]
        got = swap_all(outs[-4:-2], "dev") + swap_all(outs[-2:], "region")
    state = (disp_near, moved, veloc, summed, inverse_mass)
    last_scratch = [
        scratch(2, 3, FIRST, LANES),
        scratch(2, 3, FIRST * LANES),
        pltpu.SemaphoreType.DMA((2,)),
    ]
    halves = pl.pallas_call(
        inner_last_kernel,
        in_specs=[vector] * 5,
        out_shape=[shape((3, NLOC)), shape((3, NLOC))],
        out_specs=[raw] * 2,
        scratch_shapes=last_scratch,
        compiler_params=PARAMS,
        name="last_inner",
    )(*state)
    return pl.pallas_call(
        edge_last_kernel,
        in_specs=[vector] * 10 + [raw] * 2,
        out_shape=[shape((3, NLOC)), shape((3, NLOC))],
        out_specs=[raw] * 2,
        scratch_shapes=[scratch(4, HALF, LANES)] + last_scratch,
        input_output_aliases={10: 0, 11: 1},
        compiler_params=PARAMS,
        name="last_edge",
    )(*state, peer_index, *got, *halves)


def solution(mesh):
    in_specs = (
        P(None, ("region", "dev")),
        P(None, ("region", "dev")),
        P(None, None, ("region", "dev")),
        P(None, ("region", "dev")),
        P(None, ("region", "dev")),
        P(None, ("region", "dev")),
        P(None, ("region", "dev")),
        P(("region", "dev")),
        P(None, ("region", "dev")),
    )
    out_specs = (P(None, ("region", "dev")), P(None, ("region", "dev")))
    return jax.shard_map(body, mesh=mesh, in_specs=in_specs, out_specs=out_specs, check_vma=False)
```

```python
import functools
import math

import jax
import jax.numpy as jnp
import ml_dtypes
import numpy as np
from jax import lax
from jax.experimental import pallas as pl
from jax.experimental.pallas import tpu as pltpu
from jax.sharding import PartitionSpec as P

NODES = 125
ELEM = 320
NLOC = 20480
FCAP = 80
LANES = 128
ROWS = NLOC // LANES
FIRST = ROWS // 2
GROUPS = 20
SHARED = 4 * GROUPS
SUBSTEPS = 4
GLL_POINTS = (-1.0, -math.sqrt(3.0 / 7.0), 0.0, math.sqrt(3.0 / 7.0), 1.0)
TIME_STEP = 0.2
STEP = TIME_STEP / SUBSTEPS


def slope_rows():
    points = GLL_POINTS
    rows = []
    for row_at in range(5):
        entries = []
        for col_at in range(5):
            if row_at == col_at:
                summed = 0.0
                for other_at in range(5):
                    if other_at != row_at:
                        summed += 1.0 / (points[row_at] - points[other_at])
                entries.append(summed)
            else:
                top_prod = 1.0
                low_prod = 1.0
                for other_at in range(5):
                    if other_at != row_at:
                        top_prod *= points[row_at] - points[other_at]
                    if other_at != col_at:
                        low_prod *= points[col_at] - points[other_at]
                entries.append(top_prod / low_prod / (points[row_at] - points[col_at]))
        rows.append(entries)
    return rows


def slope_operands():
    slopes = np.array(slope_rows(), dtype=np.float32)
    eye = np.eye(5, dtype=np.float32)
    along = [
        np.kron(np.kron(slopes, eye), eye),
        np.kron(np.kron(eye, slopes), eye),
        np.kron(np.kron(eye, eye), slopes),
    ]
    grad = np.zeros((LANES, 3 * LANES), np.float32)
    back = np.zeros((3 * LANES, LANES), np.float32)
    for i, matrix in enumerate(along):
        grad[:NODES, i * LANES : i * LANES + NODES] = matrix.T
        back[i * LANES : i * LANES + NODES, :NODES] = matrix

    def terms(whole):
        high = whole.astype(ml_dtypes.bfloat16)
        return high, (whole - high.astype(np.float32)).astype(ml_dtypes.bfloat16)

    high, low = terms(grad)
    return np.concatenate([high, high, low], axis=0), np.concatenate(terms(back), axis=1)


def split_terms(whole):
    high = whole.astype(jnp.bfloat16)
    low = (whole - high.astype(jnp.float32)).astype(jnp.bfloat16)
    return high, low


def lane_pick(values, index):
    return jnp.take_along_axis(values, index, axis=1, mode="promise_in_bounds")


def one_hot_product(rows, high, low):
    both = jnp.dot(
        rows, jnp.concatenate([high, low], axis=1), preferred_element_type=jnp.float32
    )
    return both[:, : high.shape[1]] + both[:, high.shape[1] :]


def forces(shifted, jac, lam, mu, grad, back):
    count = shifted[0].shape[0]
    high, low = split_terms(jnp.concatenate(shifted, axis=0))
    slope = jnp.dot(
        jnp.concatenate([high, low, high], axis=1), grad, preferred_element_type=jnp.float32
    )
    strain = [
        [
            jac[i] * slope[c * count : (c + 1) * count, i * LANES : (i + 1) * LANES]
            for i in range(3)
        ]
        for c in range(3)
    ]
    traced = lam * (strain[0][0] + strain[1][1] + strain[2][2])
    rows = []
    for c in range(3):
        fluxes = []
        for i in range(3):
            stress = mu * (strain[c][i] + strain[i][c])
            if c == i:
                stress = stress + traced
            fluxes.append(jac[i] * stress)
        rows.append(jnp.concatenate(fluxes, axis=1))
    high, low = split_terms(jnp.concatenate(rows, axis=0))
    out = jnp.dot(high, back, preferred_element_type=jnp.float32)
    out = (
        out[:, :LANES]
        + out[:, LANES:]
        + jnp.dot(low, back[:, :LANES], preferred_element_type=jnp.float32)
    )
    return [out[c * count : (c + 1) * count] for c in range(3)]


def inverse_rows(index, turned_ref, count, missing):
    turned_ref[...] = index.astype(jnp.float32).T
    target = lax.broadcasted_iota(jnp.int32, (LANES, LANES), 0).astype(jnp.float32)
    target = target.astype(jnp.bfloat16)
    found = jnp.full((LANES, LANES), missing, jnp.bfloat16)
    for k in range(count):
        row = jnp.broadcast_to(turned_ref[k : k + 1, :], (16, LANES)).astype(jnp.bfloat16)
        row = jnp.concatenate([row] * (LANES // 16), axis=0)
        found = jnp.where(row == target, jnp.full((LANES, LANES), k, jnp.bfloat16), found)
    return found.astype(jnp.float32).T.astype(jnp.int32)


def high_half(shape):
    return lax.broadcasted_iota(jnp.int32, shape, 1) >= LANES // 2


def fine_local(moved, statics, collect, spread, grad, back):
    jac0, jac1, jac2, lam, mu, index, place = statics
    high, low = split_terms(jnp.concatenate(moved, axis=1))
    rows = one_hot_product(collect, high, low)
    upper = high_half((1, LANES))
    shifted = []
    for c in range(3):
        part = slice(c * LANES, (c + 1) * LANES)
        shifted.append(lane_pick(jnp.where(upper, rows[:FCAP, part], rows[FCAP:, part]), index))
    out = forces(shifted, (jac0, jac1, jac2), lam, mu, grad, back)
    slotted = jnp.concatenate([lane_pick(o, place) for o in out], axis=1)
    upper = lax.broadcasted_iota(jnp.int32, slotted.shape, 1) % LANES >= LANES // 2
    blank = jnp.zeros((LANES - FCAP, slotted.shape[1]), jnp.float32)
    both = jnp.concatenate(
        [jnp.where(upper, slotted, 0.0), blank, jnp.where(upper, 0.0, slotted), blank], axis=0
    )
    high, low = split_terms(both)
    return one_hot_product(spread, high, low)


def send_pair(shared, picks, odd, staged_ref, outs):
    for c, values in enumerate(shared):
        staged_ref[c] = lane_pick(values, picks)
    for c in range(len(shared)):
        part = [staged_ref[c, GROUPS * p : GROUPS * (p + 1), :] for p in range(2)]
        put = pl.ds(c * GROUPS, GROUPS)
        outs[0][put, :] = jnp.where(odd, part[1], part[0])
        outs[1][put, :] = jnp.where(odd, part[0], part[1])


def received_pair(arrived, channels, places, odd, staged_ref):
    for c in range(channels):
        got = [a[c * GROUPS : (c + 1) * GROUPS, :] for a in arrived]
        staged_ref[c, 0:GROUPS, :] = jnp.where(odd, got[1][...], got[0][...])
        staged_ref[c, GROUPS : 2 * GROUPS, :] = jnp.where(odd, got[0][...], got[1][...])
    return [lane_pick(staged_ref[c], places) for c in range(channels)]


def odd_place(axis):
    return jnp.bitwise_and(lax.axis_index(axis), 1) == 1


def peer_maps(peer_ref, first, rows_ref):
    for p in range(2):
        for j in range(GROUPS):
            at = p * GROUPS + j
            rows_ref[at : at + 1, :] = peer_ref[
                first + p : first + p + 1, j * LANES : (j + 1) * LANES
            ] & (LANES - 1)


def index_rows(conn_ref, low, count, index_ref):
    index_ref[...] = jnp.zeros_like(index_ref)
    index_ref[0:count, 0:NODES] = conn_ref[low : low + count, :] & (LANES - 1)


def value_rows(refs, low, count, value_ref):
    jac_ref, lam_ref, mu_ref, dens_ref = refs
    value_ref[:, :, LANES - 8 :] = jnp.zeros_like(value_ref[:, :, LANES - 8 :])
    sources = [jac_ref.at[0], jac_ref.at[1], jac_ref.at[2], lam_ref, mu_ref, dens_ref]
    for a, source in enumerate(sources):
        value_ref[a, 0:count, 0:NODES] = source[low : low + count, :]


def row_forces(low_row, part, disp_ref, disp_low, value_ref, index_ref, place_ref, first, grad, back, total_ref, total_low):
    upper = high_half((1, LANES))

    def paired(ref, *at):
        start = 2 * low_row - first
        return jnp.concatenate(
            [ref[(*at, pl.ds(start + odd, part, stride=2), slice(None))] for odd in range(2)],
            axis=0,
        )

    index, place = paired(index_ref), paired(place_ref)
    shifted = []
    at = low_row - disp_low
    for c in range(3):
        here = channel(disp_ref, c, at, part)
        after = channel(disp_ref, c, at + 1, part)
        shifted.append(
            lane_pick(jnp.concatenate([here, jnp.where(upper, here, after)], axis=0), index)
        )
    nodal = forces(
        shifted,
        [paired(value_ref, a) for a in range(3)],
        paired(value_ref, 3),
        paired(value_ref, 4),
        grad,
        back,
    )
    nodal.append(paired(value_ref, 5))
    at = low_row - total_low
    for c in range(4):
        spot = lane_pick(nodal[c], place)
        even, odd = spot[:part], spot[part:]
        total_ref[c, at : at + part, :] += even + jnp.where(upper, odd, 0.0)
        total_ref[c, at + 1 : at + part + 1, :] += jnp.where(upper, 0.0, odd)


def field_rows(source, low, count, out_ref):
    for j in range(count):
        row = (low + j) % ROWS
        out_ref[4 * j : 4 * j + 3, :] = source[:, row * LANES : (row + 1) * LANES]


def channel(ref, c, low, count):
    return ref[pl.ds(4 * low + c, count, stride=4), :]


EDGE = 8
HALF = 2 * GROUPS
WIDE = HALF + EDGE


def edge_part(axis, ready, sources, outs, scratches):
    disp_in, jac_ref, lam_ref, mu_ref, dens_ref, conn_ref, peer_ref, grad_ref, back_ref = sources
    base_ref, spill_ref, sends0, sends1 = outs
    (
        value_ref,
        index_ref,
        place_ref,
        turned_ref,
        disp_ref,
        peer_rows_ref,
        staged_ref,
        total_ref,
    ) = scratches
    first = FIRST if axis == "dev" else FIRST + HALF
    low_row = first - EDGE
    total_ref[...] = jnp.zeros_like(total_ref)
    ready(0)
    index_rows(conn_ref, 2 * low_row, 2 * WIDE, index_ref)
    place_ref[...] = inverse_rows(index_ref[...], turned_ref, NODES, LANES - 1)
    ready(1)
    field_rows(disp_in, low_row, WIDE + 1, disp_ref)
    peer_maps(peer_ref, 0 if axis == "dev" else 2, peer_rows_ref)
    ready(2)
    value_rows((jac_ref, lam_ref, mu_ref, dens_ref), 2 * low_row, 2 * WIDE, value_ref)
    row_forces(
        low_row,
        WIDE,
        disp_ref,
        low_row,
        value_ref,
        index_ref,
        place_ref,
        2 * low_row,
        grad_ref[...],
        back_ref[...],
        total_ref,
        low_row,
    )
    for c in range(4):
        base_ref[c] = total_ref[c, EDGE:WIDE, :]
        spill_ref[c] = total_ref[c, WIDE : WIDE + 8, :]
    send_pair(
        [base_ref[c] for c in range(4)],
        peer_rows_ref[...],
        odd_place(axis),
        staged_ref,
        (sends0, sends1),
    )


def dev_edge_kernel(*refs):
    raw, kept, outs, scratches = refs[:11], refs[11:22], refs[22:26], refs[26:34]
    sems = refs[34]
    disp_in, veloc_in, jac_in, lam_in, mu_in, dens_in, conn_in, peer_in, grad_in, back_in = raw[:10]
    disp, veloc, jac, lam, mu, dens, conn, peer, grad, back = kept[:10]
    low = 2 * (FIRST - EDGE)
    mine, lower, upper = pl.ds(low, 2 * WIDE), pl.ds(0, low), pl.ds(low + 2 * WIDE, ELEM - low - 2 * WIDE)
    steps = [
        [(conn_in.at[mine, :], conn.at[mine, :])],
        [(disp_in, disp), (peer_in, peer)],
        [(jac_in.at[:, mine, :], jac.at[:, mine, :]), (grad_in, grad)]
        + [(x.at[mine, :], y.at[mine, :]) for x, y in ((lam_in, lam), (mu_in, mu), (dens_in, dens))]
        + [(back_in, back)],
        [(veloc_in, veloc), (raw[10], kept[10])]
        + [(jac_in.at[:, part, :], jac.at[:, part, :]) for part in (upper, lower)]
        + [
            (x.at[part, :], y.at[part, :])
            for part in (upper, lower)
            for x, y in ((lam_in, lam), (mu_in, mu), (dens_in, dens), (conn_in, conn))
        ],
    ]
    copies, count = [], 0
    for step in steps:
        group = []
        for source, target in step:
            group.append(pltpu.make_async_copy(source, target, sems.at[count]))
            count += 1
        copies.append(group)
    for group in copies:
        for copy in group:
            copy.start()

    def ready(step):
        for copy in copies[step]:
            copy.wait()

    edge_part("dev", ready, (disp,) + tuple(kept[2:10]), outs, scratches)
    ready(3)


def region_edge_kernel(*refs):
    edge_part("region", lambda step: None, refs[:9], refs[10:14], refs[14:22])


def inner_kernel(
    slots_in,
    slot_row_ref,
    disp_in,
    veloc_in,
    jac_ref,
    lam_ref,
    mu_ref,
    dens_ref,
    conn_ref,
    peer_ref,
    spill_in,
    grad_ref,
    back_ref,
    veloc_ref,
    base_ref,
    fixed_ref,
    index_out,
    collect_ref,
    spread_ref,
    peer_index_ref,
    value_ref,
    index_ref,
    place_ref,
    turned_ref,
    disp_ref,
    veloc_rows_ref,
    peer_rows_ref,
    total_ref,
    spread_wide_ref,
    slots_ref,
    slots_sem,
):
    slots_copy = pltpu.make_async_copy(slots_in, slots_ref, slots_sem)
    slots_copy.start()
    field_rows(disp_in, 0, FIRST + 1, disp_ref)
    index_rows(conn_ref, 0, ELEM, index_ref)
    value_rows((jac_ref, lam_ref, mu_ref, dens_ref), 0, ELEM, value_ref)
    value_ref[:, ELEM:, :] = jnp.zeros_like(value_ref[:, ELEM:, :])
    place_ref[0:LANES, :] = inverse_rows(index_ref[0:LANES, :], turned_ref, NODES, LANES - 1)
    total_ref[...] = jnp.zeros_like(total_ref)
    for c in range(4):
        total_ref[c, 0:1, :] = spill_in[c, 0:1, :]

    def add_rows(low_row):
        row_forces(
            low_row,
            FIRST,
            disp_ref,
            0,
            value_ref,
            index_ref,
            place_ref,
            0,
            grad_ref[...],
            back_ref[...],
            total_ref,
            0,
        )

    field_rows(veloc_in, 0, ROWS, veloc_rows_ref)
    for c in range(3):
        veloc_ref[c] = channel(veloc_rows_ref, c, 0, ROWS)
    for half in range(2):
        peer_maps(peer_ref, 2 * half, peer_rows_ref.at[pl.ds(half * HALF, HALF), :])
    peer_rows_ref[SHARED:, :] = jnp.zeros((LANES - SHARED, LANES), jnp.int32)
    peer_index_ref[0] = peer_rows_ref[0:SHARED, :]
    peer_index_ref[1] = inverse_rows(peer_rows_ref[...], turned_ref, LANES, 0)[0:SHARED]
    slots_copy.wait()
    for s in range(FCAP):
        e = slots_ref[s]
        for a in range(5):
            fixed_ref[a, s : s + 1, :] = value_ref[a, pl.ds(e, 1), :]
        index_out[0, s : s + 1, :] = index_ref[pl.ds(e, 1), :]
    tail = ELEM // 2 - LANES
    both = jnp.concatenate(
        [
            index_ref[LANES : LANES + tail, :],
            index_out[0],
            jnp.zeros((LANES - tail - FCAP, LANES), jnp.int32),
        ],
        axis=0,
    )
    found = inverse_rows(both, turned_ref, NODES, LANES - 1)
    place_ref[LANES : LANES + tail, :] = found[0:tail]
    index_out[1] = found[tail : tail + FCAP]
    rows = lax.broadcasted_iota(jnp.int32, (ROWS, FCAP), 0)
    slot_row = slot_row_ref[...]
    second = lax.shift_right_logical(slot_row + 1, 1)
    second = jnp.where(second == ROWS, 0, second)
    spread_wide_ref[...] = jnp.zeros_like(spread_wide_ref)
    spread_wide_ref[0:ROWS, 0:FCAP] = jnp.where(
        lax.shift_right_logical(slot_row, 1) == rows, 1.0, 0.0
    )
    spread_wide_ref[0:ROWS, LANES : LANES + FCAP] = jnp.where(second == rows, 1.0, 0.0)
    spread_ref[...] = spread_wide_ref[0:ROWS, :].astype(jnp.bfloat16)
    for half in range(2):
        turned = spread_wide_ref[:, half * LANES : (half + 1) * LANES].T
        collect_ref[half * FCAP : (half + 1) * FCAP, :] = turned[:FCAP, :ROWS].astype(
            jnp.bfloat16
        )
    add_rows(0)
    for c in range(4):
        base_ref[c] = total_ref[c, 0:FIRST, :]


def received_rows(arrived, channels, peer_index_ref, staged_ref):
    dev = received_pair(
        arrived[:2], channels, peer_index_ref[1, 0:HALF, :], odd_place("dev"), staged_ref
    )
    region = received_pair(
        arrived[2:], channels, peer_index_ref[1, HALF:, :], odd_place("region"), staged_ref
    )
    return [jnp.concatenate([d, r], axis=0) for d, r in zip(dev, region)]


def whole_base(c, inner_ref, dev_ref, region_ref):
    return jnp.concatenate([inner_ref[c], dev_ref[c], region_ref[c]], axis=0)


def middle_kernel(
    opening,
    moved_ref,
    veloc_ref,
    inner_ref,
    dev_ref,
    region_ref,
    summed_ref,
    inverse_ref,
    fixed_ref,
    index_ref,
    collect_ref,
    spread_ref,
    peer_index_ref,
    got0,
    got1,
    got2,
    got3,
    grad_ref,
    back_ref,
    moved_out,
    veloc_out,
    summed_out,
    *rest,
):
    if opening:
        inverse_out, sends0, sends1, sends2, sends3, staged_ref = rest
    else:
        sends0, sends1, sends2, sends3, staged_ref = rest
    placed = received_rows(
        (got0, got1, got2, got3), 4 if opening else 3, peer_index_ref, staged_ref
    )
    if opening:
        mass = whole_base(3, inner_ref, dev_ref, region_ref)
        inverse_out[0:FIRST, :] = 1.0 / mass[:FIRST]
        inverse_out[FIRST:, :] = 1.0 / (mass[FIRST:] + placed[3])
        inverse_mass = inverse_out[...]
    else:
        inverse_mass = inverse_ref[...]
    base = [whole_base(c, inner_ref, dev_ref, region_ref) for c in range(3)]
    moved = []
    for c in range(3):
        local = base[c] if opening else summed_ref[c]
        force = jnp.concatenate([local[:FIRST], local[FIRST:] + placed[c]], axis=0)
        v = veloc_ref[c] - STEP * (inverse_mass * force)
        moved.append(STEP * v if opening else moved_ref[c] + STEP * v)
        moved_out[c] = moved[c]
        veloc_out[c] = v
    fine = fine_local(
        moved,
        [fixed_ref[a] for a in range(5)] + [index_ref[a] for a in range(2)],
        collect_ref[...],
        spread_ref[...],
        grad_ref[...],
        back_ref[...],
    )
    for c in range(3):
        summed_out[c] = base[c] + fine[:, c * LANES : (c + 1) * LANES]
    for axis, at, outs in (("dev", 0, (sends0, sends1)), ("region", HALF, (sends2, sends3))):
        send_pair(
            [summed_out[c, FIRST + at : FIRST + at + HALF, :] for c in range(3)],
            peer_index_ref[0, at : at + HALF, :],
            odd_place(axis),
            staged_ref,
            outs,
        )


def last_rows(low, count, force, refs, outs, scratches):
    disp_in, moved_ref, veloc_ref, inverse_ref = refs
    rows_ref, lines_ref, sems = scratches
    part = pl.ds(low, count)
    for c in range(3):
        v = veloc_ref[c, part, :] - STEP * (inverse_ref[part, :] * force[c])
        rows_ref[0, pl.ds(c, count, stride=4), :] = moved_ref[c, part, :] + STEP * v
        rows_ref[1, pl.ds(c, count, stride=4), :] = v
    copies = []
    for which in (1, 0):
        for j in range(count):
            cols = slice(j * LANES, (j + 1) * LANES)
            whole = slice((low + j) * LANES, (low + j + 1) * LANES)
            row = rows_ref[which, 4 * j : 4 * j + 3, :]
            if which == 0:
                row = disp_in[:, whole] + row
            lines_ref[which, :, cols] = row
        copy = pltpu.make_async_copy(
            lines_ref.at[which],
            outs[which].at[:, pl.ds(low * LANES, count * LANES)],
            sems.at[which],
        )
        copy.start()
        copies.append(copy)
    for copy in copies:
        copy.wait()


def inner_last_kernel(
    disp_in, moved_ref, veloc_ref, summed_ref, inverse_ref, disp_out, veloc_out, *scratches
):
    last_rows(
        0,
        FIRST,
        [summed_ref[c, :FIRST, :] for c in range(3)],
        (disp_in, moved_ref, veloc_ref, inverse_ref),
        (disp_out, veloc_out),
        scratches,
    )


def edge_last_kernel(
    disp_in,
    moved_ref,
    veloc_ref,
    summed_ref,
    inverse_ref,
    peer_index_ref,
    got0,
    got1,
    got2,
    got3,
    disp_half,
    veloc_half,
    disp_out,
    veloc_out,
    staged_ref,
    *scratches,
):
    placed = received_rows((got0, got1, got2, got3), 3, peer_index_ref, staged_ref)
    last_rows(
        FIRST,
        FIRST,
        [summed_ref[c, FIRST:, :] + placed[c] for c in range(3)],
        (disp_in, moved_ref, veloc_ref, inverse_ref),
        (disp_out, veloc_out),
        scratches,
    )


def swap_pairs(count, colour):
    pairs = []
    for low in range(colour, count, 2):
        high = (low + 1) % count
        pairs += [(low, high), (high, low)]
    return pairs


def swap_all(sends, axis):
    return [
        lax.ppermute(sent, axis, swap_pairs(lax.axis_size(axis), colour))
        for colour, sent in zip((1, 0), sends)
    ]


def shape(dims, kind=jnp.float32):
    return jax.ShapeDtypeStruct(dims, kind)


def scratch(*dims, kind=jnp.float32):
    return pltpu.VMEM(dims, kind)


PARAMS = pltpu.CompilerParams(vmem_limit_bytes=48 * 1024 * 1024)


def body(
    disp_start,
    veloc_start,
    jacobian,
    lame_lambda,
    lame_mu,
    density,
    connect,
    fine_slots,
    peer_nodes,
):
    grad_np, back_np = slope_operands()
    grad, back = jnp.asarray(grad_np), jnp.asarray(back_np)
    vector = pl.BlockSpec(memory_space=pltpu.VMEM)
    field = shape((3, ROWS, LANES))
    elements = (
        jnp.transpose(jacobian, (0, 2, 1)),
        lame_lambda.T,
        lame_mu.T,
        density.T,
        connect.T,
    )

    def sends(channels, count):
        return [shape((channels * GROUPS, LANES))] * count

    got, bases = [], []
    raw = pl.BlockSpec(memory_space=pltpu.HBM)
    slot_row = fine_slots.reshape(1, FCAP)
    arguments = (disp_start, veloc_start, *elements, peer_nodes, grad, back, slot_row)
    edge_outs = [shape((4, HALF, LANES)), shape((4, 8, LANES))] + sends(4, 2)
    edge_scratch = [
        scratch(6, LANES, LANES),
        scratch(LANES, LANES, kind=jnp.int32),
        scratch(LANES, LANES, kind=jnp.int32),
        scratch(LANES, LANES),
        scratch(4 * (WIDE + 8), LANES),
        scratch(HALF, LANES, kind=jnp.int32),
        scratch(4, HALF, LANES),
        scratch(4, WIDE + 8, LANES),
    ]
    outs = pl.pallas_call(
        dev_edge_kernel,
        in_specs=[raw] * 11,
        out_shape=[shape(x.shape, x.dtype) for x in arguments] + edge_outs,
        out_specs=[vector] * 15,
        scratch_shapes=edge_scratch + [pltpu.SemaphoreType.DMA((21,))],
        compiler_params=PARAMS,
        name="edge_dev",
    )(*[pltpu.with_memory_space_constraint(x, pltpu.HBM) for x in arguments])
    disp_near, veloc_near, *near, slots_near = outs[:11]
    base, order, send0, send1 = outs[11:]
    bases.append(base)
    got += swap_all((send0, send1), "dev")
    base, spill, send0, send1 = pl.pallas_call(
        region_edge_kernel,
        in_specs=[vector] * 10,
        out_shape=edge_outs,
        out_specs=[vector] * 4,
        scratch_shapes=edge_scratch,
        compiler_params=PARAMS,
        name="edge_region",
    )(disp_near, *near, order)
    bases.append(base)
    got += swap_all((send0, send1), "region")
    veloc, inner, fixed, index, collect, spread, peer_index = pl.pallas_call(
        inner_kernel,
        in_specs=[raw] + [vector] * 12,
        out_shape=[
            field,
            shape((4, FIRST, LANES)),
            shape((5, FCAP, LANES)),
            shape((2, FCAP, LANES), jnp.int32),
            shape((2 * FCAP, ROWS), jnp.bfloat16),
            shape((ROWS, 2 * LANES), jnp.bfloat16),
            shape((2, SHARED, LANES), jnp.int32),
        ],
        out_specs=[vector] * 7,
        scratch_shapes=[
            scratch(6, ELEM + 8, LANES),
            scratch(ELEM + 8, LANES, kind=jnp.int32),
            scratch(ELEM // 2, LANES, kind=jnp.int32),
            scratch(LANES, LANES),
            scratch(4 * (FIRST + 8), LANES),
            scratch(4 * ROWS, LANES),
            scratch(LANES, LANES, kind=jnp.int32),
            scratch(4, FIRST + 8, LANES),
            scratch(2 * LANES, 2 * LANES),
            pltpu.SMEM((FCAP,), jnp.int32),
            pltpu.SemaphoreType.DMA(()),
        ],
        compiler_params=PARAMS,
        name="inner",
    )(
        pltpu.with_memory_space_constraint(fine_slots, pltpu.HBM),
        slots_near,
        disp_near,
        veloc_near,
        *near[:6],
        spill,
        *near[6:],
    )
    inverse_mass, moved, summed = peer_index, peer_index, peer_index
    for substep in range(SUBSTEPS - 1):
        opening = substep == 0
        extra = [shape((ROWS, LANES))] if opening else []
        outs = pl.pallas_call(
            functools.partial(middle_kernel, opening),
            in_specs=[vector] * 18,
            out_shape=[field, field, field] + extra + sends(3, 4),
            out_specs=[vector] * (7 + len(extra)),
            scratch_shapes=[scratch(4, HALF, LANES)],
            compiler_params=PARAMS,
            name="middle",
        )(
            moved,
            veloc,
            inner,
            *bases,
            summed,
            inverse_mass,
            fixed,
            index,
            collect,
            spread,
            peer_index,
            *got,
            grad,
            back,
        )
        moved, veloc, summed = outs[:3]
        if opening:
            inverse_mass = outs[3]
        got = swap_all(outs[-4:-2], "dev") + swap_all(outs[-2:], "region")
    state = (disp_near, moved, veloc, summed, inverse_mass)
    last_scratch = [
        scratch(2, 4 * FIRST, LANES),
        scratch(2, 3, FIRST * LANES),
        pltpu.SemaphoreType.DMA((2,)),
    ]
    halves = pl.pallas_call(
        inner_last_kernel,
        in_specs=[vector] * 5,
        out_shape=[shape((3, NLOC)), shape((3, NLOC))],
        out_specs=[raw] * 2,
        scratch_shapes=last_scratch,
        compiler_params=PARAMS,
        name="last_inner",
    )(*state)
    return pl.pallas_call(
        edge_last_kernel,
        in_specs=[vector] * 10 + [raw] * 2,
        out_shape=[shape((3, NLOC)), shape((3, NLOC))],
        out_specs=[raw] * 2,
        scratch_shapes=[scratch(4, HALF, LANES)] + last_scratch,
        input_output_aliases={10: 0, 11: 1},
        compiler_params=PARAMS,
        name="last_edge",
    )(*state, peer_index, *got, *halves)


def solution(mesh):
    in_specs = (
        P(None, ("region", "dev")),
        P(None, ("region", "dev")),
        P(None, None, ("region", "dev")),
        P(None, ("region", "dev")),
        P(None, ("region", "dev")),
        P(None, ("region", "dev")),
        P(None, ("region", "dev")),
        P(("region", "dev")),
        P(None, ("region", "dev")),
    )
    out_specs = (P(None, ("region", "dev")), P(None, ("region", "dev")))
    return jax.shard_map(body, mesh=mesh, in_specs=in_specs, out_specs=out_specs, check_vma=False)
```

```python
import functools
import math

import jax
import jax.numpy as jnp
import ml_dtypes
import numpy as np
from jax import lax
from jax.experimental import pallas as pl
from jax.experimental.pallas import tpu as pltpu
from jax.sharding import PartitionSpec as P

NODES = 125
ELEM = 320
NLOC = 20480
FCAP = 80
LANES = 128
ROWS = NLOC // LANES
FIRST = ROWS // 2
GROUPS = 20
SHARED = 4 * GROUPS
SUBSTEPS = 4
GLL_POINTS = (-1.0, -math.sqrt(3.0 / 7.0), 0.0, math.sqrt(3.0 / 7.0), 1.0)
TIME_STEP = 0.2
STEP = TIME_STEP / SUBSTEPS


def slope_rows():
    points = GLL_POINTS
    rows = []
    for row_at in range(5):
        entries = []
        for col_at in range(5):
            if row_at == col_at:
                summed = 0.0
                for other_at in range(5):
                    if other_at != row_at:
                        summed += 1.0 / (points[row_at] - points[other_at])
                entries.append(summed)
            else:
                top_prod = 1.0
                low_prod = 1.0
                for other_at in range(5):
                    if other_at != row_at:
                        top_prod *= points[row_at] - points[other_at]
                    if other_at != col_at:
                        low_prod *= points[col_at] - points[other_at]
                entries.append(top_prod / low_prod / (points[row_at] - points[col_at]))
        rows.append(entries)
    return rows


def slope_operands():
    slopes = np.array(slope_rows(), dtype=np.float32)
    eye = np.eye(5, dtype=np.float32)
    along = [
        np.kron(np.kron(slopes, eye), eye),
        np.kron(np.kron(eye, slopes), eye),
        np.kron(np.kron(eye, eye), slopes),
    ]
    grad = np.zeros((LANES, 3 * LANES), np.float32)
    back = np.zeros((3 * LANES, LANES), np.float32)
    for i, matrix in enumerate(along):
        grad[:NODES, i * LANES : i * LANES + NODES] = matrix.T
        back[i * LANES : i * LANES + NODES, :NODES] = matrix

    def terms(whole):
        high = whole.astype(ml_dtypes.bfloat16)
        return high, (whole - high.astype(np.float32)).astype(ml_dtypes.bfloat16)

    high, low = terms(grad)
    return np.concatenate([high, high, low], axis=0), np.concatenate(terms(back), axis=1)


def split_terms(whole):
    high = whole.astype(jnp.bfloat16)
    low = (whole - high.astype(jnp.float32)).astype(jnp.bfloat16)
    return high, low


def lane_pick(values, index):
    return jnp.take_along_axis(values, index, axis=1, mode="promise_in_bounds")


def one_hot_product(rows, high, low):
    both = jnp.dot(
        rows, jnp.concatenate([high, low], axis=1), preferred_element_type=jnp.float32
    )
    return both[:, : high.shape[1]] + both[:, high.shape[1] :]


def forces(shifted, jac, lam, mu, grad, back):
    count = shifted[0].shape[0]
    high, low = split_terms(jnp.concatenate(shifted, axis=0))
    slope = jnp.dot(
        jnp.concatenate([high, low, high], axis=1), grad, preferred_element_type=jnp.float32
    )
    strain = [
        [
            jac[i] * slope[c * count : (c + 1) * count, i * LANES : (i + 1) * LANES]
            for i in range(3)
        ]
        for c in range(3)
    ]
    traced = lam * (strain[0][0] + strain[1][1] + strain[2][2])
    rows = []
    for c in range(3):
        fluxes = []
        for i in range(3):
            stress = mu * (strain[c][i] + strain[i][c])
            if c == i:
                stress = stress + traced
            fluxes.append(jac[i] * stress)
        rows.append(jnp.concatenate(fluxes, axis=1))
    high, low = split_terms(jnp.concatenate(rows, axis=0))
    out = jnp.dot(high, back, preferred_element_type=jnp.float32)
    out = (
        out[:, :LANES]
        + out[:, LANES:]
        + jnp.dot(low, back[:, :LANES], preferred_element_type=jnp.float32)
    )
    return [out[c * count : (c + 1) * count] for c in range(3)]


def inverse_rows(index, turned_ref, count, missing):
    turned_ref[...] = index.astype(jnp.float32).T
    target = lax.broadcasted_iota(jnp.int32, (LANES, LANES), 0).astype(jnp.float32)
    target = target.astype(jnp.bfloat16)
    found = jnp.full((LANES, LANES), missing, jnp.bfloat16)
    for k in range(count):
        row = jnp.broadcast_to(turned_ref[k : k + 1, :], (16, LANES)).astype(jnp.bfloat16)
        row = jnp.concatenate([row] * (LANES // 16), axis=0)
        found = jnp.where(row == target, jnp.full((LANES, LANES), k, jnp.bfloat16), found)
    return found.astype(jnp.float32).T.astype(jnp.int32)


def high_half(shape):
    return lax.broadcasted_iota(jnp.int32, shape, 1) >= LANES // 2


def fine_local(moved, statics, collect, spread, grad, back):
    jac0, jac1, jac2, lam, mu, index, place = statics
    high, low = split_terms(jnp.concatenate(moved, axis=1))
    rows = one_hot_product(collect, high, low)
    upper = high_half((1, LANES))
    shifted = []
    for c in range(3):
        part = slice(c * LANES, (c + 1) * LANES)
        shifted.append(lane_pick(jnp.where(upper, rows[:FCAP, part], rows[FCAP:, part]), index))
    out = forces(shifted, (jac0, jac1, jac2), lam, mu, grad, back)
    slotted = jnp.concatenate([lane_pick(o, place) for o in out], axis=1)
    upper = lax.broadcasted_iota(jnp.int32, slotted.shape, 1) % LANES >= LANES // 2
    blank = jnp.zeros((LANES - FCAP, slotted.shape[1]), jnp.float32)
    both = jnp.concatenate(
        [jnp.where(upper, slotted, 0.0), blank, jnp.where(upper, 0.0, slotted), blank], axis=0
    )
    high, low = split_terms(both)
    return one_hot_product(spread, high, low)


def send_pair(shared, picks, odd, staged_ref, outs):
    for c, values in enumerate(shared):
        staged_ref[c, 0:HALF, :] = lane_pick(values, picks)
    for c in range(len(shared)):
        part = [staged_ref[c, GROUPS * p : GROUPS * (p + 1), :] for p in range(2)]
        put = pl.ds(c * GROUPS, GROUPS)
        outs[0][put, :] = jnp.where(odd, part[1], part[0])
        outs[1][put, :] = jnp.where(odd, part[0], part[1])


def received_pair(arrived, channels, places, odd, staged_ref):
    for c in range(channels):
        got = [a[c * GROUPS : (c + 1) * GROUPS, :] for a in arrived]
        staged_ref[c, 0:GROUPS, :] = jnp.where(odd, got[1][...], got[0][...])
        staged_ref[c, GROUPS : 2 * GROUPS, :] = jnp.where(odd, got[0][...], got[1][...])
    return [lane_pick(staged_ref[c, 0:HALF, :], places) for c in range(channels)]


def odd_place(axis):
    return jnp.bitwise_and(lax.axis_index(axis), 1) == 1


def peer_maps(peer_ref, first, rows_ref):
    for p in range(2):
        for j in range(GROUPS):
            at = p * GROUPS + j
            rows_ref[at : at + 1, :] = peer_ref[
                first + p : first + p + 1, j * LANES : (j + 1) * LANES
            ] & (LANES - 1)


def index_rows(conn_ref, low, count, index_ref):
    index_ref[...] = jnp.zeros_like(index_ref)
    index_ref[0:count, 0:NODES] = conn_ref[low : low + count, :] & (LANES - 1)


def value_rows(refs, low, count, value_ref):
    jac_ref, lam_ref, mu_ref, dens_ref = refs
    value_ref[:, :, LANES - 8 :] = jnp.zeros_like(value_ref[:, :, LANES - 8 :])
    sources = [jac_ref.at[0], jac_ref.at[1], jac_ref.at[2], lam_ref, mu_ref, dens_ref]
    for a, source in enumerate(sources):
        value_ref[a, 0:count, 0:NODES] = source[low : low + count, :]


def row_forces(low_row, part, disp_ref, disp_low, value_ref, index_ref, place_ref, first, grad, back, total_ref, total_low):
    upper = high_half((1, LANES))

    def paired(ref, *at):
        start = 2 * low_row - first
        return jnp.concatenate(
            [ref[(*at, pl.ds(start + odd, part, stride=2), slice(None))] for odd in range(2)],
            axis=0,
        )

    index, place = paired(index_ref), paired(place_ref)
    shifted = []
    at = low_row - disp_low
    for c in range(3):
        here = channel(disp_ref, c, at, part)
        after = channel(disp_ref, c, at + 1, part)
        shifted.append(
            lane_pick(jnp.concatenate([here, jnp.where(upper, here, after)], axis=0), index)
        )
    nodal = forces(
        shifted,
        [paired(value_ref, a) for a in range(3)],
        paired(value_ref, 3),
        paired(value_ref, 4),
        grad,
        back,
    )
    nodal.append(paired(value_ref, 5))
    at = low_row - total_low
    for c in range(4):
        spot = lane_pick(nodal[c], place)
        even, odd = spot[:part], spot[part:]
        total_ref[c, at : at + part, :] += even + jnp.where(upper, odd, 0.0)
        total_ref[c, at + 1 : at + part + 1, :] += jnp.where(upper, 0.0, odd)


def field_rows(source, low, count, out_ref):
    for j in range(count):
        row = (low + j) % ROWS
        out_ref[4 * j : 4 * j + 3, :] = source[:, row * LANES : (row + 1) * LANES]


def channel(ref, c, low, count):
    return ref[pl.ds(4 * low + c, count, stride=4), :]


EDGE = 8
HALF = 2 * GROUPS
WIDE = HALF + EDGE


def edge_part(axis, ready, sources, outs, scratches):
    disp_in, jac_ref, lam_ref, mu_ref, dens_ref, conn_ref, peer_ref, grad_ref, back_ref = sources
    base_ref, spill_ref, sends0, sends1 = outs
    (
        value_ref,
        index_ref,
        place_ref,
        turned_ref,
        disp_ref,
        peer_rows_ref,
        staged_ref,
        total_ref,
    ) = scratches
    first = FIRST if axis == "dev" else FIRST + HALF
    low_row = first - EDGE
    total_ref[...] = jnp.zeros_like(total_ref)
    ready(0)
    index_rows(conn_ref, 2 * low_row, 2 * WIDE, index_ref)
    place_ref[...] = inverse_rows(index_ref[...], turned_ref, NODES, LANES - 1)
    ready(1)
    field_rows(disp_in, low_row, WIDE + 1, disp_ref)
    peer_maps(peer_ref, 0 if axis == "dev" else 2, peer_rows_ref)
    ready(2)
    value_rows((jac_ref, lam_ref, mu_ref, dens_ref), 2 * low_row, 2 * WIDE, value_ref)
    row_forces(
        low_row,
        WIDE,
        disp_ref,
        low_row,
        value_ref,
        index_ref,
        place_ref,
        2 * low_row,
        grad_ref[...],
        back_ref[...],
        total_ref,
        low_row,
    )
    for c in range(4):
        base_ref[c] = total_ref[c, EDGE:WIDE, :]
        spill_ref[c] = total_ref[c, WIDE : WIDE + 8, :]
    send_pair(
        [base_ref[c] for c in range(4)],
        peer_rows_ref[...],
        odd_place(axis),
        staged_ref,
        (sends0, sends1),
    )


def dev_edge_kernel(*refs):
    raw, kept, outs, scratches = refs[:11], refs[11:22], refs[22:26], refs[26:34]
    sems = refs[34]
    disp_in, veloc_in, jac_in, lam_in, mu_in, dens_in, conn_in, peer_in, grad_in, back_in = raw[:10]
    disp, veloc, jac, lam, mu, dens, conn, peer, grad, back = kept[:10]
    low = 2 * (FIRST - EDGE)
    mine, lower, upper = pl.ds(low, 2 * WIDE), pl.ds(0, low), pl.ds(low + 2 * WIDE, ELEM - low - 2 * WIDE)
    steps = [
        [(conn_in.at[mine, :], conn.at[mine, :])],
        [(disp_in, disp), (peer_in, peer)],
        [(jac_in.at[:, mine, :], jac.at[:, mine, :]), (grad_in, grad)]
        + [(x.at[mine, :], y.at[mine, :]) for x, y in ((lam_in, lam), (mu_in, mu), (dens_in, dens))]
        + [(back_in, back)],
        [(veloc_in, veloc), (raw[10], kept[10])]
        + [(jac_in.at[:, part, :], jac.at[:, part, :]) for part in (upper, lower)]
        + [
            (x.at[part, :], y.at[part, :])
            for part in (upper, lower)
            for x, y in ((lam_in, lam), (mu_in, mu), (dens_in, dens), (conn_in, conn))
        ],
    ]
    copies, count = [], 0
    for step in steps:
        group = []
        for source, target in step:
            group.append(pltpu.make_async_copy(source, target, sems.at[count]))
            count += 1
        copies.append(group)
    for group in copies:
        for copy in group:
            copy.start()

    def ready(step):
        for copy in copies[step]:
            copy.wait()

    edge_part("dev", ready, (disp,) + tuple(kept[2:10]), outs, scratches)
    ready(3)


def region_edge_kernel(*refs):
    edge_part("region", lambda step: None, refs[:9], refs[10:14], refs[14:22])


def inner_kernel(
    slots_in,
    slot_row_ref,
    disp_in,
    veloc_in,
    jac_ref,
    lam_ref,
    mu_ref,
    dens_ref,
    conn_ref,
    peer_ref,
    spill_in,
    grad_ref,
    back_ref,
    veloc_ref,
    base_ref,
    fixed_ref,
    index_out,
    collect_ref,
    spread_ref,
    peer_index_ref,
    value_ref,
    index_ref,
    place_ref,
    turned_ref,
    disp_ref,
    veloc_rows_ref,
    peer_rows_ref,
    total_ref,
    spread_wide_ref,
    slots_ref,
    slots_sem,
):
    slots_copy = pltpu.make_async_copy(slots_in, slots_ref, slots_sem)
    slots_copy.start()
    field_rows(disp_in, 0, FIRST + 1, disp_ref)
    index_rows(conn_ref, 0, ELEM, index_ref)
    value_rows((jac_ref, lam_ref, mu_ref, dens_ref), 0, ELEM, value_ref)
    value_ref[:, ELEM:, :] = jnp.zeros_like(value_ref[:, ELEM:, :])
    place_ref[0:LANES, :] = inverse_rows(index_ref[0:LANES, :], turned_ref, NODES, LANES - 1)
    total_ref[...] = jnp.zeros_like(total_ref)
    for c in range(4):
        total_ref[c, 0:1, :] = spill_in[c, 0:1, :]

    def add_rows(low_row):
        row_forces(
            low_row,
            FIRST,
            disp_ref,
            0,
            value_ref,
            index_ref,
            place_ref,
            0,
            grad_ref[...],
            back_ref[...],
            total_ref,
            0,
        )

    field_rows(veloc_in, 0, ROWS, veloc_rows_ref)
    for c in range(3):
        veloc_ref[c] = channel(veloc_rows_ref, c, 0, ROWS)
    for half in range(2):
        peer_maps(peer_ref, 2 * half, peer_rows_ref.at[pl.ds(half * HALF, HALF), :])
    peer_rows_ref[SHARED:, :] = jnp.zeros((LANES - SHARED, LANES), jnp.int32)
    peer_index_ref[0] = peer_rows_ref[0:SHARED, :]
    peer_index_ref[1] = inverse_rows(peer_rows_ref[...], turned_ref, LANES, 0)[0:SHARED]
    slots_copy.wait()
    for s in range(FCAP):
        e = slots_ref[s]
        for a in range(5):
            fixed_ref[a, s : s + 1, :] = value_ref[a, pl.ds(e, 1), :]
        index_out[0, s : s + 1, :] = index_ref[pl.ds(e, 1), :]
    tail = ELEM // 2 - LANES
    both = jnp.concatenate(
        [
            index_ref[LANES : LANES + tail, :],
            index_out[0],
            jnp.zeros((LANES - tail - FCAP, LANES), jnp.int32),
        ],
        axis=0,
    )
    found = inverse_rows(both, turned_ref, NODES, LANES - 1)
    place_ref[LANES : LANES + tail, :] = found[0:tail]
    index_out[1] = found[tail : tail + FCAP]
    rows = lax.broadcasted_iota(jnp.int32, (ROWS, FCAP), 0)
    slot_row = slot_row_ref[...]
    second = lax.shift_right_logical(slot_row + 1, 1)
    second = jnp.where(second == ROWS, 0, second)
    spread_wide_ref[...] = jnp.zeros_like(spread_wide_ref)
    spread_wide_ref[0:ROWS, 0:FCAP] = jnp.where(
        lax.shift_right_logical(slot_row, 1) == rows, 1.0, 0.0
    )
    spread_wide_ref[0:ROWS, LANES : LANES + FCAP] = jnp.where(second == rows, 1.0, 0.0)
    spread_ref[...] = spread_wide_ref[0:ROWS, :].astype(jnp.bfloat16)
    for half in range(2):
        turned = spread_wide_ref[:, half * LANES : (half + 1) * LANES].T
        collect_ref[half * FCAP : (half + 1) * FCAP, :] = turned[:FCAP, :ROWS].astype(
            jnp.bfloat16
        )
    add_rows(0)
    for c in range(4):
        base_ref[c] = total_ref[c, 0:FIRST, :]


def received_rows(arrived, channels, peer_index_ref, staged_ref):
    dev = received_pair(
        arrived[:2], channels, peer_index_ref[1, 0:HALF, :], odd_place("dev"), staged_ref
    )
    region = received_pair(
        arrived[2:], channels, peer_index_ref[1, HALF:, :], odd_place("region"), staged_ref
    )
    return [jnp.concatenate([d, r], axis=0) for d, r in zip(dev, region)]


def whole_base(c, inner_ref, dev_ref, region_ref):
    return jnp.concatenate([inner_ref[c], dev_ref[c], region_ref[c]], axis=0)


def middle_kernel(
    opening,
    moved_ref,
    veloc_ref,
    inner_ref,
    dev_ref,
    region_ref,
    summed_ref,
    inverse_ref,
    fixed_ref,
    index_ref,
    collect_ref,
    spread_ref,
    peer_index_ref,
    got0,
    got1,
    got2,
    got3,
    grad_ref,
    back_ref,
    moved_out,
    veloc_out,
    summed_out,
    *rest,
):
    if opening:
        inverse_out, sends0, sends1, sends2, sends3, staged_ref = rest
    else:
        sends0, sends1, sends2, sends3, staged_ref = rest
    placed = received_rows(
        (got0, got1, got2, got3), 4 if opening else 3, peer_index_ref, staged_ref
    )
    if opening:
        mass = whole_base(3, inner_ref, dev_ref, region_ref)
        inverse_out[0:FIRST, :] = 1.0 / mass[:FIRST]
        inverse_out[FIRST:, :] = 1.0 / (mass[FIRST:] + placed[3])
        inverse_mass = inverse_out[...]
    else:
        inverse_mass = inverse_ref[...]
    base = [whole_base(c, inner_ref, dev_ref, region_ref) for c in range(3)]
    moved = []
    for c in range(3):
        local = base[c] if opening else summed_ref[c]
        force = jnp.concatenate([local[:FIRST], local[FIRST:] + placed[c]], axis=0)
        v = veloc_ref[c] - STEP * (inverse_mass * force)
        moved.append(STEP * v if opening else moved_ref[c] + STEP * v)
        moved_out[c] = moved[c]
        veloc_out[c] = v
    fine = fine_local(
        moved,
        [fixed_ref[a] for a in range(5)] + [index_ref[a] for a in range(2)],
        collect_ref[...],
        spread_ref[...],
        grad_ref[...],
        back_ref[...],
    )
    for c in range(3):
        summed_out[c] = base[c] + fine[:, c * LANES : (c + 1) * LANES]
    for axis, at, outs in (("dev", 0, (sends0, sends1)), ("region", HALF, (sends2, sends3))):
        send_pair(
            [summed_out[c, FIRST + at : FIRST + at + HALF, :] for c in range(3)],
            peer_index_ref[0, at : at + HALF, :],
            odd_place(axis),
            staged_ref,
            outs,
        )


def last_rows(low, count, force, refs, outs, scratches):
    disp_in, moved_ref, veloc_ref, inverse_ref = refs
    rows_ref, lines_ref, sems = scratches
    part = pl.ds(low, count)
    for c in range(3):
        v = veloc_ref[c, part, :] - STEP * (inverse_ref[part, :] * force[c])
        rows_ref[0, pl.ds(c, count, stride=4), :] = moved_ref[c, part, :] + STEP * v
        rows_ref[1, pl.ds(c, count, stride=4), :] = v
    copies = []
    for which in (1, 0):
        for j in range(count):
            cols = slice(j * LANES, (j + 1) * LANES)
            whole = slice((low + j) * LANES, (low + j + 1) * LANES)
            row = rows_ref[which, 4 * j : 4 * j + 3, :]
            if which == 0:
                row = disp_in[:, whole] + row
            lines_ref[which, :, cols] = row
        copy = pltpu.make_async_copy(
            lines_ref.at[which],
            outs[which].at[:, pl.ds(low * LANES, count * LANES)],
            sems.at[which],
        )
        copy.start()
        copies.append(copy)
    for copy in copies:
        copy.wait()


def inner_last_kernel(
    disp_in, moved_ref, veloc_ref, summed_ref, inverse_ref, disp_out, veloc_out, *scratches
):
    last_rows(
        0,
        FIRST,
        [summed_ref[c, :FIRST, :] for c in range(3)],
        (disp_in, moved_ref, veloc_ref, inverse_ref),
        (disp_out, veloc_out),
        scratches,
    )


def edge_last_kernel(
    disp_in,
    moved_ref,
    veloc_ref,
    summed_ref,
    inverse_ref,
    peer_index_ref,
    got0,
    got1,
    got2,
    got3,
    disp_half,
    veloc_half,
    disp_out,
    veloc_out,
    staged_ref,
    *scratches,
):
    placed = received_rows((got0, got1, got2, got3), 3, peer_index_ref, staged_ref)
    last_rows(
        FIRST,
        FIRST,
        [summed_ref[c, FIRST:, :] + placed[c] for c in range(3)],
        (disp_in, moved_ref, veloc_ref, inverse_ref),
        (disp_out, veloc_out),
        scratches,
    )


def swap_pairs(count, colour):
    pairs = []
    for low in range(colour, count, 2):
        high = (low + 1) % count
        pairs += [(low, high), (high, low)]
    return pairs


def swap_all(sends, axis):
    return [
        lax.ppermute(sent, axis, swap_pairs(lax.axis_size(axis), colour))
        for colour, sent in zip((1, 0), sends)
    ]


def shape(dims, kind=jnp.float32):
    return jax.ShapeDtypeStruct(dims, kind)


def scratch(*dims, kind=jnp.float32):
    return pltpu.VMEM(dims, kind)


PARAMS = pltpu.CompilerParams(vmem_limit_bytes=48 * 1024 * 1024)


def body(
    disp_start,
    veloc_start,
    jacobian,
    lame_lambda,
    lame_mu,
    density,
    connect,
    fine_slots,
    peer_nodes,
):
    grad_np, back_np = slope_operands()
    grad, back = jnp.asarray(grad_np), jnp.asarray(back_np)
    vector = pl.BlockSpec(memory_space=pltpu.VMEM)
    field = shape((3, ROWS, LANES))
    elements = (
        jnp.transpose(jacobian, (0, 2, 1)),
        lame_lambda.T,
        lame_mu.T,
        density.T,
        connect.T,
    )

    def sends(channels, count):
        return [shape((-(-channels * GROUPS // 8) * 8, LANES))] * count

    got, bases = [], []
    raw = pl.BlockSpec(memory_space=pltpu.HBM)
    slot_row = fine_slots.reshape(1, FCAP)
    arguments = (disp_start, veloc_start, *elements, peer_nodes, grad, back, slot_row)
    edge_outs = [shape((4, HALF, LANES)), shape((4, 8, LANES))] + sends(4, 2)
    edge_scratch = [
        scratch(6, LANES, LANES),
        scratch(LANES, LANES, kind=jnp.int32),
        scratch(LANES, LANES, kind=jnp.int32),
        scratch(LANES, LANES),
        scratch(4 * (WIDE + 8), LANES),
        scratch(HALF, LANES, kind=jnp.int32),
        scratch(4, HALF + 8, LANES),
        scratch(4, WIDE + 8, LANES),
    ]
    outs = pl.pallas_call(
        dev_edge_kernel,
        in_specs=[raw] * 11,
        out_shape=[shape(x.shape, x.dtype) for x in arguments] + edge_outs,
        out_specs=[vector] * 15,
        scratch_shapes=edge_scratch + [pltpu.SemaphoreType.DMA((21,))],
        compiler_params=PARAMS,
        name="edge_dev",
    )(*[pltpu.with_memory_space_constraint(x, pltpu.HBM) for x in arguments])
    disp_near, veloc_near, *near, slots_near = outs[:11]
    base, order, send0, send1 = outs[11:]
    bases.append(base)
    got += swap_all((send0, send1), "dev")
    base, spill, send0, send1 = pl.pallas_call(
        region_edge_kernel,
        in_specs=[vector] * 10,
        out_shape=edge_outs,
        out_specs=[vector] * 4,
        scratch_shapes=edge_scratch,
        compiler_params=PARAMS,
        name="edge_region",
    )(disp_near, *near, order)
    bases.append(base)
    got += swap_all((send0, send1), "region")
    veloc, inner, fixed, index, collect, spread, peer_index = pl.pallas_call(
        inner_kernel,
        in_specs=[raw] + [vector] * 12,
        out_shape=[
            field,
            shape((4, FIRST, LANES)),
            shape((5, FCAP, LANES)),
            shape((2, FCAP, LANES), jnp.int32),
            shape((2 * FCAP, ROWS), jnp.bfloat16),
            shape((ROWS, 2 * LANES), jnp.bfloat16),
            shape((2, SHARED, LANES), jnp.int32),
        ],
        out_specs=[vector] * 7,
        scratch_shapes=[
            scratch(6, ELEM + 8, LANES),
            scratch(ELEM + 8, LANES, kind=jnp.int32),
            scratch(ELEM // 2 + 8, LANES, kind=jnp.int32),
            scratch(LANES, LANES),
            scratch(4 * (FIRST + 8), LANES),
            scratch(4 * ROWS + 8, LANES),
            scratch(LANES, LANES, kind=jnp.int32),
            scratch(4, FIRST + 8, LANES),
            scratch(2 * LANES, 2 * LANES),
            pltpu.SMEM((FCAP,), jnp.int32),
            pltpu.SemaphoreType.DMA(()),
        ],
        compiler_params=PARAMS,
        name="inner",
    )(
        pltpu.with_memory_space_constraint(fine_slots, pltpu.HBM),
        slots_near,
        disp_near,
        veloc_near,
        *near[:6],
        spill,
        *near[6:],
    )
    inverse_mass, moved, summed = peer_index, peer_index, peer_index
    for substep in range(SUBSTEPS - 1):
        opening = substep == 0
        extra = [shape((ROWS, LANES))] if opening else []
        outs = pl.pallas_call(
            functools.partial(middle_kernel, opening),
            in_specs=[vector] * 18,
            out_shape=[field, field, field] + extra + sends(3, 4),
            out_specs=[vector] * (7 + len(extra)),
            scratch_shapes=[scratch(4, HALF + 8, LANES)],
            compiler_params=PARAMS,
            name="middle",
        )(
            moved,
            veloc,
            inner,
            *bases,
            summed,
            inverse_mass,
            fixed,
            index,
            collect,
            spread,
            peer_index,
            *got,
            grad,
            back,
        )
        moved, veloc, summed = outs[:3]
        if opening:
            inverse_mass = outs[3]
        got = swap_all(outs[-4:-2], "dev") + swap_all(outs[-2:], "region")
    state = (disp_near, moved, veloc, summed, inverse_mass)
    last_scratch = [
        scratch(2, 4 * FIRST + 8, LANES),
        scratch(2, 3, FIRST * LANES),
        pltpu.SemaphoreType.DMA((2,)),
    ]
    halves = pl.pallas_call(
        inner_last_kernel,
        in_specs=[vector] * 5,
        out_shape=[shape((3, NLOC)), shape((3, NLOC))],
        out_specs=[raw] * 2,
        scratch_shapes=last_scratch,
        compiler_params=PARAMS,
        name="last_inner",
    )(*state)
    return pl.pallas_call(
        edge_last_kernel,
        in_specs=[vector] * 10 + [raw] * 2,
        out_shape=[shape((3, NLOC)), shape((3, NLOC))],
        out_specs=[raw] * 2,
        scratch_shapes=[scratch(4, HALF + 8, LANES)] + last_scratch,
        input_output_aliases={10: 0, 11: 1},
        compiler_params=PARAMS,
        name="last_edge",
    )(*state, peer_index, *got, *halves)


def solution(mesh):
    in_specs = (
        P(None, ("region", "dev")),
        P(None, ("region", "dev")),
        P(None, None, ("region", "dev")),
        P(None, ("region", "dev")),
        P(None, ("region", "dev")),
        P(None, ("region", "dev")),
        P(None, ("region", "dev")),
        P(("region", "dev")),
        P(None, ("region", "dev")),
    )
    out_specs = (P(None, ("region", "dev")), P(None, ("region", "dev")))
    return jax.shard_map(body, mesh=mesh, in_specs=in_specs, out_specs=out_specs, check_vma=False)
```

```python
import functools
import math

import jax
import jax.numpy as jnp
import ml_dtypes
import numpy as np
from jax import lax
from jax.experimental import pallas as pl
from jax.experimental.pallas import tpu as pltpu
from jax.sharding import PartitionSpec as P

NODES = 125
ELEM = 320
NLOC = 20480
FCAP = 80
LANES = 128
ROWS = NLOC // LANES
FIRST = ROWS // 2
GROUPS = 20
SHARED = 4 * GROUPS
SUBSTEPS = 4
GLL_POINTS = (-1.0, -math.sqrt(3.0 / 7.0), 0.0, math.sqrt(3.0 / 7.0), 1.0)
TIME_STEP = 0.2
STEP = TIME_STEP / SUBSTEPS


def slope_rows():
    points = GLL_POINTS
    rows = []
    for row_at in range(5):
        entries = []
        for col_at in range(5):
            if row_at == col_at:
                summed = 0.0
                for other_at in range(5):
                    if other_at != row_at:
                        summed += 1.0 / (points[row_at] - points[other_at])
                entries.append(summed)
            else:
                top_prod = 1.0
                low_prod = 1.0
                for other_at in range(5):
                    if other_at != row_at:
                        top_prod *= points[row_at] - points[other_at]
                    if other_at != col_at:
                        low_prod *= points[col_at] - points[other_at]
                entries.append(top_prod / low_prod / (points[row_at] - points[col_at]))
        rows.append(entries)
    return rows


def slope_operands():
    slopes = np.array(slope_rows(), dtype=np.float32)
    eye = np.eye(5, dtype=np.float32)
    along = [
        np.kron(np.kron(slopes, eye), eye),
        np.kron(np.kron(eye, slopes), eye),
        np.kron(np.kron(eye, eye), slopes),
    ]
    grad = np.zeros((LANES, 3 * LANES), np.float32)
    back = np.zeros((3 * LANES, LANES), np.float32)
    for i, matrix in enumerate(along):
        grad[:NODES, i * LANES : i * LANES + NODES] = matrix.T
        back[i * LANES : i * LANES + NODES, :NODES] = matrix

    def terms(whole):
        high = whole.astype(ml_dtypes.bfloat16)
        return high, (whole - high.astype(np.float32)).astype(ml_dtypes.bfloat16)

    high, low = terms(grad)
    return np.concatenate([high, high, low], axis=0), np.concatenate(terms(back), axis=1)


def split_terms(whole):
    high = whole.astype(jnp.bfloat16)
    low = (whole - high.astype(jnp.float32)).astype(jnp.bfloat16)
    return high, low


def lane_pick(values, index):
    return jnp.take_along_axis(values, index, axis=1, mode="promise_in_bounds")


def one_hot_product(rows, high, low):
    both = jnp.dot(
        rows, jnp.concatenate([high, low], axis=1), preferred_element_type=jnp.float32
    )
    return both[:, : high.shape[1]] + both[:, high.shape[1] :]


def forces(shifted, jac, lam, mu, grad, back):
    count = shifted[0].shape[0]
    high, low = split_terms(jnp.concatenate(shifted, axis=0))
    slope = jnp.dot(
        jnp.concatenate([high, low, high], axis=1), grad, preferred_element_type=jnp.float32
    )
    strain = [
        [
            jac[i] * slope[c * count : (c + 1) * count, i * LANES : (i + 1) * LANES]
            for i in range(3)
        ]
        for c in range(3)
    ]
    traced = lam * (strain[0][0] + strain[1][1] + strain[2][2])
    rows = []
    for c in range(3):
        fluxes = []
        for i in range(3):
            stress = mu * (strain[c][i] + strain[i][c])
            if c == i:
                stress = stress + traced
            fluxes.append(jac[i] * stress)
        rows.append(jnp.concatenate(fluxes, axis=1))
    high, low = split_terms(jnp.concatenate(rows, axis=0))
    out = jnp.dot(high, back, preferred_element_type=jnp.float32)
    out = (
        out[:, :LANES]
        + out[:, LANES:]
        + jnp.dot(low, back[:, :LANES], preferred_element_type=jnp.float32)
    )
    return [out[c * count : (c + 1) * count] for c in range(3)]


def inverse_rows(index, turned_ref, count, missing):
    turned_ref[...] = index.astype(jnp.float32).T
    target = lax.broadcasted_iota(jnp.int32, (LANES, LANES), 0).astype(jnp.float32)
    target = target.astype(jnp.bfloat16)
    found = jnp.full((LANES, LANES), missing, jnp.bfloat16)
    for k in range(count):
        row = jnp.broadcast_to(turned_ref[k : k + 1, :], (16, LANES)).astype(jnp.bfloat16)
        row = jnp.concatenate([row] * (LANES // 16), axis=0)
        found = jnp.where(row == target, jnp.full((LANES, LANES), k, jnp.bfloat16), found)
    return found.astype(jnp.float32).T.astype(jnp.int32)


def high_half(shape):
    return lax.broadcasted_iota(jnp.int32, shape, 1) >= LANES // 2


def fine_local(moved, statics, collect, spread, grad, back):
    jac0, jac1, jac2, lam, mu, index, place = statics
    high, low = split_terms(jnp.concatenate(moved, axis=1))
    rows = one_hot_product(collect, high, low)
    upper = high_half((1, LANES))
    shifted = []
    for c in range(3):
        part = slice(c * LANES, (c + 1) * LANES)
        shifted.append(lane_pick(jnp.where(upper, rows[:FCAP, part], rows[FCAP:, part]), index))
    out = forces(shifted, (jac0, jac1, jac2), lam, mu, grad, back)
    slotted = jnp.concatenate([lane_pick(o, place) for o in out], axis=1)
    upper = lax.broadcasted_iota(jnp.int32, slotted.shape, 1) % LANES >= LANES // 2
    blank = jnp.zeros((LANES - FCAP, slotted.shape[1]), jnp.float32)
    both = jnp.concatenate(
        [jnp.where(upper, slotted, 0.0), blank, jnp.where(upper, 0.0, slotted), blank], axis=0
    )
    high, low = split_terms(both)
    return one_hot_product(spread, high, low)


def send_pair(shared, picks, odd, staged_ref, outs):
    for c, values in enumerate(shared):
        staged_ref[c, 0:HALF, :] = lane_pick(values, picks)
    for c in range(len(shared)):
        part = [staged_ref[c, GROUPS * p : GROUPS * (p + 1), :] for p in range(2)]
        put = pl.ds(c * GROUPS, GROUPS)
        outs[0][put, :] = jnp.where(odd, part[1], part[0])
        outs[1][put, :] = jnp.where(odd, part[0], part[1])


def received_pair(arrived, channels, places, odd, staged_ref):
    for c in range(channels):
        got = [a[c * GROUPS : (c + 1) * GROUPS, :] for a in arrived]
        staged_ref[c, 0:GROUPS, :] = jnp.where(odd, got[1][...], got[0][...])
        staged_ref[c, GROUPS : 2 * GROUPS, :] = jnp.where(odd, got[0][...], got[1][...])
    return [lane_pick(staged_ref[c, 0:HALF, :], places) for c in range(channels)]


def odd_place(axis):
    return jnp.bitwise_and(lax.axis_index(axis), 1) == 1


def peer_maps(peer_ref, first, rows_ref):
    for p in range(2):
        for j in range(GROUPS):
            at = p * GROUPS + j
            rows_ref[at : at + 1, :] = peer_ref[
                first + p : first + p + 1, j * LANES : (j + 1) * LANES
            ] & (LANES - 1)


def index_rows(conn_ref, low, count, index_ref):
    index_ref[...] = jnp.zeros_like(index_ref)
    index_ref[0:count, 0:NODES] = conn_ref[low : low + count, :] & (LANES - 1)


def value_rows(refs, low, count, value_ref):
    jac_ref, lam_ref, mu_ref, dens_ref = refs
    value_ref[:, :, LANES - 8 :] = jnp.zeros_like(value_ref[:, :, LANES - 8 :])
    sources = [jac_ref.at[0], jac_ref.at[1], jac_ref.at[2], lam_ref, mu_ref, dens_ref]
    for a, source in enumerate(sources):
        value_ref[a, 0:count, 0:NODES] = source[low : low + count, :]


def row_forces(low_row, part, disp_ref, disp_low, value_ref, index_ref, place_ref, first, grad, back, total_ref, total_low):
    upper = high_half((1, LANES))

    def paired(ref, *at):
        start = 2 * low_row - first
        return jnp.concatenate(
            [ref[(*at, pl.ds(start + odd, part, stride=2), slice(None))] for odd in range(2)],
            axis=0,
        )

    index, place = paired(index_ref), paired(place_ref)
    shifted = []
    at = low_row - disp_low
    for c in range(3):
        here = channel(disp_ref, c, at, part)
        after = channel(disp_ref, c, at + 1, part)
        shifted.append(
            lane_pick(jnp.concatenate([here, jnp.where(upper, here, after)], axis=0), index)
        )
    nodal = forces(
        shifted,
        [paired(value_ref, a) for a in range(3)],
        paired(value_ref, 3),
        paired(value_ref, 4),
        grad,
        back,
    )
    nodal.append(paired(value_ref, 5))
    at = low_row - total_low
    for c in range(4):
        spot = lane_pick(nodal[c], place)
        even, odd = spot[:part], spot[part:]
        total_ref[c, at : at + part, :] += even + jnp.where(upper, odd, 0.0)
        total_ref[c, at + 1 : at + part + 1, :] += jnp.where(upper, 0.0, odd)


def field_rows(source, low, count, out_ref):
    for j in range(count):
        row = (low + j) % ROWS
        out_ref[4 * j : 4 * j + 3, :] = source[:, row * LANES : (row + 1) * LANES]


def channel(ref, c, low, count):
    return ref[pl.ds(4 * low + c, count, stride=4), :]


EDGE = 8
HALF = 2 * GROUPS
WIDE = HALF + EDGE


def edge_part(axis, ready, sources, outs, scratches):
    disp_in, jac_ref, lam_ref, mu_ref, dens_ref, conn_ref, peer_ref, grad_ref, back_ref = sources
    base_ref, spill_ref, sends0, sends1 = outs
    (
        value_ref,
        index_ref,
        place_ref,
        turned_ref,
        disp_ref,
        peer_rows_ref,
        staged_ref,
        total_ref,
    ) = scratches
    first = FIRST if axis == "dev" else FIRST + HALF
    low_row = first - EDGE
    total_ref[...] = jnp.zeros_like(total_ref)
    ready(0)
    index_rows(conn_ref, 2 * low_row, 2 * WIDE, index_ref)
    place_ref[...] = inverse_rows(index_ref[...], turned_ref, NODES, LANES - 1)
    ready(1)
    field_rows(disp_in, low_row, WIDE + 1, disp_ref)
    peer_maps(peer_ref, 0 if axis == "dev" else 2, peer_rows_ref)
    ready(2)
    value_rows((jac_ref, lam_ref, mu_ref, dens_ref), 2 * low_row, 2 * WIDE, value_ref)
    row_forces(
        low_row,
        WIDE,
        disp_ref,
        low_row,
        value_ref,
        index_ref,
        place_ref,
        2 * low_row,
        grad_ref[...],
        back_ref[...],
        total_ref,
        low_row,
    )
    for c in range(4):
        base_ref[c] = total_ref[c, EDGE:WIDE, :]
        spill_ref[c] = total_ref[c, WIDE : WIDE + 8, :]
    send_pair(
        [base_ref[c] for c in range(4)],
        peer_rows_ref[...],
        odd_place(axis),
        staged_ref,
        (sends0, sends1),
    )


def dev_edge_kernel(*refs):
    raw, kept, outs, scratches = refs[:11], refs[11:22], refs[22:26], refs[26:34]
    sems = refs[34]
    disp_in, veloc_in, jac_in, lam_in, mu_in, dens_in, conn_in, peer_in, grad_in, back_in = raw[:10]
    disp, veloc, jac, lam, mu, dens, conn, peer, grad, back = kept[:10]
    low = 2 * (FIRST - EDGE)
    mine, lower, upper = pl.ds(low, 2 * WIDE), pl.ds(0, low), pl.ds(low + 2 * WIDE, ELEM - low - 2 * WIDE)
    start, stop = (FIRST - EDGE) * LANES, (FIRST + HALF + 1) * LANES
    strip, above, below = pl.ds(start, stop - start), pl.ds(stop, NLOC - stop), pl.ds(0, start)
    steps = [
        [(conn_in.at[mine, :], conn.at[mine, :])],
        [(disp_in.at[:, strip], disp.at[:, strip]), (peer_in, peer)],
        [(jac_in.at[:, mine, :], jac.at[:, mine, :]), (grad_in, grad)]
        + [(x.at[mine, :], y.at[mine, :]) for x, y in ((lam_in, lam), (mu_in, mu), (dens_in, dens))]
        + [(back_in, back)],
        [(disp_in.at[:, part], disp.at[:, part]) for part in (above, below)]
        + [(veloc_in, veloc), (raw[10], kept[10])]
        + [(jac_in.at[:, part, :], jac.at[:, part, :]) for part in (upper, lower)]
        + [
            (x.at[part, :], y.at[part, :])
            for part in (upper, lower)
            for x, y in ((lam_in, lam), (mu_in, mu), (dens_in, dens), (conn_in, conn))
        ],
    ]
    copies, count = [], 0
    for step in steps:
        group = []
        for source, target in step:
            group.append(pltpu.make_async_copy(source, target, sems.at[count]))
            count += 1
        copies.append(group)
    for group in copies:
        for copy in group:
            copy.start()

    def ready(step):
        for copy in copies[step]:
            copy.wait()

    edge_part("dev", ready, (disp,) + tuple(kept[2:10]), outs, scratches)
    ready(3)


def region_edge_kernel(*refs):
    edge_part("region", lambda step: None, refs[:9], refs[10:14], refs[14:22])


def inner_kernel(
    slots_in,
    slot_row_ref,
    disp_in,
    veloc_in,
    jac_ref,
    lam_ref,
    mu_ref,
    dens_ref,
    conn_ref,
    peer_ref,
    spill_in,
    grad_ref,
    back_ref,
    veloc_ref,
    base_ref,
    fixed_ref,
    index_out,
    collect_ref,
    spread_ref,
    peer_index_ref,
    value_ref,
    index_ref,
    place_ref,
    turned_ref,
    disp_ref,
    veloc_rows_ref,
    peer_rows_ref,
    total_ref,
    spread_wide_ref,
    slots_ref,
    slots_sem,
):
    slots_copy = pltpu.make_async_copy(slots_in, slots_ref, slots_sem)
    slots_copy.start()
    field_rows(disp_in, 0, FIRST + 1, disp_ref)
    index_rows(conn_ref, 0, ELEM, index_ref)
    value_rows((jac_ref, lam_ref, mu_ref, dens_ref), 0, ELEM, value_ref)
    value_ref[:, ELEM:, :] = jnp.zeros_like(value_ref[:, ELEM:, :])
    place_ref[0:LANES, :] = inverse_rows(index_ref[0:LANES, :], turned_ref, NODES, LANES - 1)
    total_ref[...] = jnp.zeros_like(total_ref)
    for c in range(4):
        total_ref[c, 0:1, :] = spill_in[c, 0:1, :]

    def add_rows(low_row):
        row_forces(
            low_row,
            FIRST,
            disp_ref,
            0,
            value_ref,
            index_ref,
            place_ref,
            0,
            grad_ref[...],
            back_ref[...],
            total_ref,
            0,
        )

    field_rows(veloc_in, 0, ROWS, veloc_rows_ref)
    for c in range(3):
        veloc_ref[c] = channel(veloc_rows_ref, c, 0, ROWS)
    for half in range(2):
        peer_maps(peer_ref, 2 * half, peer_rows_ref.at[pl.ds(half * HALF, HALF), :])
    peer_rows_ref[SHARED:, :] = jnp.zeros((LANES - SHARED, LANES), jnp.int32)
    peer_index_ref[0] = peer_rows_ref[0:SHARED, :]
    peer_index_ref[1] = inverse_rows(peer_rows_ref[...], turned_ref, LANES, 0)[0:SHARED]
    slots_copy.wait()
    for s in range(FCAP):
        e = slots_ref[s]
        for a in range(5):
            fixed_ref[a, s : s + 1, :] = value_ref[a, pl.ds(e, 1), :]
        index_out[0, s : s + 1, :] = index_ref[pl.ds(e, 1), :]
    tail = ELEM // 2 - LANES
    both = jnp.concatenate(
        [
            index_ref[LANES : LANES + tail, :],
            index_out[0],
            jnp.zeros((LANES - tail - FCAP, LANES), jnp.int32),
        ],
        axis=0,
    )
    found = inverse_rows(both, turned_ref, NODES, LANES - 1)
    place_ref[LANES : LANES + tail, :] = found[0:tail]
    index_out[1] = found[tail : tail + FCAP]
    rows = lax.broadcasted_iota(jnp.int32, (ROWS, FCAP), 0)
    slot_row = slot_row_ref[...]
    second = lax.shift_right_logical(slot_row + 1, 1)
    second = jnp.where(second == ROWS, 0, second)
    spread_wide_ref[...] = jnp.zeros_like(spread_wide_ref)
    spread_wide_ref[0:ROWS, 0:FCAP] = jnp.where(
        lax.shift_right_logical(slot_row, 1) == rows, 1.0, 0.0
    )
    spread_wide_ref[0:ROWS, LANES : LANES + FCAP] = jnp.where(second == rows, 1.0, 0.0)
    spread_ref[...] = spread_wide_ref[0:ROWS, :].astype(jnp.bfloat16)
    for half in range(2):
        turned = spread_wide_ref[:, half * LANES : (half + 1) * LANES].T
        collect_ref[half * FCAP : (half + 1) * FCAP, :] = turned[:FCAP, :ROWS].astype(
            jnp.bfloat16
        )
    add_rows(0)
    for c in range(4):
        base_ref[c] = total_ref[c, 0:FIRST, :]


def received_rows(arrived, channels, peer_index_ref, staged_ref):
    dev = received_pair(
        arrived[:2], channels, peer_index_ref[1, 0:HALF, :], odd_place("dev"), staged_ref
    )
    region = received_pair(
        arrived[2:], channels, peer_index_ref[1, HALF:, :], odd_place("region"), staged_ref
    )
    return [jnp.concatenate([d, r], axis=0) for d, r in zip(dev, region)]


def whole_base(c, inner_ref, dev_ref, region_ref):
    return jnp.concatenate([inner_ref[c], dev_ref[c], region_ref[c]], axis=0)


def middle_kernel(
    opening,
    moved_ref,
    veloc_ref,
    inner_ref,
    dev_ref,
    region_ref,
    summed_ref,
    inverse_ref,
    fixed_ref,
    index_ref,
    collect_ref,
    spread_ref,
    peer_index_ref,
    got0,
    got1,
    got2,
    got3,
    grad_ref,
    back_ref,
    moved_out,
    veloc_out,
    summed_out,
    *rest,
):
    if opening:
        inverse_out, sends0, sends1, sends2, sends3, staged_ref = rest
    else:
        sends0, sends1, sends2, sends3, staged_ref = rest
    placed = received_rows(
        (got0, got1, got2, got3), 4 if opening else 3, peer_index_ref, staged_ref
    )
    if opening:
        mass = whole_base(3, inner_ref, dev_ref, region_ref)
        inverse_out[0:FIRST, :] = 1.0 / mass[:FIRST]
        inverse_out[FIRST:, :] = 1.0 / (mass[FIRST:] + placed[3])
        inverse_mass = inverse_out[...]
    else:
        inverse_mass = inverse_ref[...]
    base = [whole_base(c, inner_ref, dev_ref, region_ref) for c in range(3)]
    moved = []
    for c in range(3):
        local = base[c] if opening else summed_ref[c]
        force = jnp.concatenate([local[:FIRST], local[FIRST:] + placed[c]], axis=0)
        v = veloc_ref[c] - STEP * (inverse_mass * force)
        moved.append(STEP * v if opening else moved_ref[c] + STEP * v)
        moved_out[c] = moved[c]
        veloc_out[c] = v
    fine = fine_local(
        moved,
        [fixed_ref[a] for a in range(5)] + [index_ref[a] for a in range(2)],
        collect_ref[...],
        spread_ref[...],
        grad_ref[...],
        back_ref[...],
    )
    for c in range(3):
        summed_out[c] = base[c] + fine[:, c * LANES : (c + 1) * LANES]
    for axis, at, outs in (("dev", 0, (sends0, sends1)), ("region", HALF, (sends2, sends3))):
        send_pair(
            [summed_out[c, FIRST + at : FIRST + at + HALF, :] for c in range(3)],
            peer_index_ref[0, at : at + HALF, :],
            odd_place(axis),
            staged_ref,
            outs,
        )


def last_rows(low, count, force, refs, outs, scratches):
    disp_in, moved_ref, veloc_ref, inverse_ref = refs
    rows_ref, lines_ref, sems = scratches
    part = pl.ds(low, count)
    for c in range(3):
        v = veloc_ref[c, part, :] - STEP * (inverse_ref[part, :] * force[c])
        rows_ref[0, pl.ds(c, count, stride=4), :] = moved_ref[c, part, :] + STEP * v
        rows_ref[1, pl.ds(c, count, stride=4), :] = v
    copies = []
    for which in (1, 0):
        for j in range(count):
            cols = slice(j * LANES, (j + 1) * LANES)
            whole = slice((low + j) * LANES, (low + j + 1) * LANES)
            row = rows_ref[which, 4 * j : 4 * j + 3, :]
            if which == 0:
                row = disp_in[:, whole] + row
            lines_ref[which, :, cols] = row
        copy = pltpu.make_async_copy(
            lines_ref.at[which],
            outs[which].at[:, pl.ds(low * LANES, count * LANES)],
            sems.at[which],
        )
        copy.start()
        copies.append(copy)
    for copy in copies:
        copy.wait()


def inner_last_kernel(
    disp_in, moved_ref, veloc_ref, summed_ref, inverse_ref, disp_out, veloc_out, *scratches
):
    last_rows(
        0,
        FIRST,
        [summed_ref[c, :FIRST, :] for c in range(3)],
        (disp_in, moved_ref, veloc_ref, inverse_ref),
        (disp_out, veloc_out),
        scratches,
    )


def edge_last_kernel(
    disp_in,
    moved_ref,
    veloc_ref,
    summed_ref,
    inverse_ref,
    peer_index_ref,
    got0,
    got1,
    got2,
    got3,
    disp_half,
    veloc_half,
    disp_out,
    veloc_out,
    staged_ref,
    *scratches,
):
    placed = received_rows((got0, got1, got2, got3), 3, peer_index_ref, staged_ref)
    last_rows(
        FIRST,
        FIRST,
        [summed_ref[c, FIRST:, :] + placed[c] for c in range(3)],
        (disp_in, moved_ref, veloc_ref, inverse_ref),
        (disp_out, veloc_out),
        scratches,
    )


def swap_pairs(count, colour):
    pairs = []
    for low in range(colour, count, 2):
        high = (low + 1) % count
        pairs += [(low, high), (high, low)]
    return pairs


def swap_all(sends, axis):
    return [
        lax.ppermute(sent, axis, swap_pairs(lax.axis_size(axis), colour))
        for colour, sent in zip((1, 0), sends)
    ]


def shape(dims, kind=jnp.float32):
    return jax.ShapeDtypeStruct(dims, kind)


def scratch(*dims, kind=jnp.float32):
    return pltpu.VMEM(dims, kind)


PARAMS = pltpu.CompilerParams(vmem_limit_bytes=48 * 1024 * 1024)


def body(
    disp_start,
    veloc_start,
    jacobian,
    lame_lambda,
    lame_mu,
    density,
    connect,
    fine_slots,
    peer_nodes,
):
    grad_np, back_np = slope_operands()
    grad, back = jnp.asarray(grad_np), jnp.asarray(back_np)
    vector = pl.BlockSpec(memory_space=pltpu.VMEM)
    field = shape((3, ROWS, LANES))
    elements = (
        jnp.transpose(jacobian, (0, 2, 1)),
        lame_lambda.T,
        lame_mu.T,
        density.T,
        connect.T,
    )

    def sends(channels, count):
        return [shape((-(-channels * GROUPS // 8) * 8, LANES))] * count

    got, bases = [], []
    raw = pl.BlockSpec(memory_space=pltpu.HBM)
    slot_row = fine_slots.reshape(1, FCAP)
    arguments = (disp_start, veloc_start, *elements, peer_nodes, grad, back, slot_row)
    edge_outs = [shape((4, HALF, LANES)), shape((4, 8, LANES))] + sends(4, 2)
    edge_scratch = [
        scratch(6, LANES, LANES),
        scratch(LANES, LANES, kind=jnp.int32),
        scratch(LANES, LANES, kind=jnp.int32),
        scratch(LANES, LANES),
        scratch(4 * (WIDE + 8), LANES),
        scratch(HALF, LANES, kind=jnp.int32),
        scratch(4, HALF + 8, LANES),
        scratch(4, WIDE + 8, LANES),
    ]
    outs = pl.pallas_call(
        dev_edge_kernel,
        in_specs=[raw] * 11,
        out_shape=[shape(x.shape, x.dtype) for x in arguments] + edge_outs,
        out_specs=[vector] * 15,
        scratch_shapes=edge_scratch + [pltpu.SemaphoreType.DMA((23,))],
        compiler_params=PARAMS,
        name="edge_dev",
    )(*[pltpu.with_memory_space_constraint(x, pltpu.HBM) for x in arguments])
    disp_near, veloc_near, *near, slots_near = outs[:11]
    base, order, send0, send1 = outs[11:]
    bases.append(base)
    got += swap_all((send0, send1), "dev")
    base, spill, send0, send1 = pl.pallas_call(
        region_edge_kernel,
        in_specs=[vector] * 10,
        out_shape=edge_outs,
        out_specs=[vector] * 4,
        scratch_shapes=edge_scratch,
        compiler_params=PARAMS,
        name="edge_region",
    )(disp_near, *near, order)
    bases.append(base)
    got += swap_all((send0, send1), "region")
    veloc, inner, fixed, index, collect, spread, peer_index = pl.pallas_call(
        inner_kernel,
        in_specs=[raw] + [vector] * 12,
        out_shape=[
            field,
            shape((4, FIRST, LANES)),
            shape((5, FCAP, LANES)),
            shape((2, FCAP, LANES), jnp.int32),
            shape((2 * FCAP, ROWS), jnp.bfloat16),
            shape((ROWS, 2 * LANES), jnp.bfloat16),
            shape((2, SHARED, LANES), jnp.int32),
        ],
        out_specs=[vector] * 7,
        scratch_shapes=[
            scratch(6, ELEM + 8, LANES),
            scratch(ELEM + 8, LANES, kind=jnp.int32),
            scratch(ELEM // 2 + 8, LANES, kind=jnp.int32),
            scratch(LANES, LANES),
            scratch(4 * (FIRST + 8), LANES),
            scratch(4 * ROWS + 8, LANES),
            scratch(LANES, LANES, kind=jnp.int32),
            scratch(4, FIRST + 8, LANES),
            scratch(2 * LANES, 2 * LANES),
            pltpu.SMEM((FCAP,), jnp.int32),
            pltpu.SemaphoreType.DMA(()),
        ],
        compiler_params=PARAMS,
        name="inner",
    )(
        pltpu.with_memory_space_constraint(fine_slots, pltpu.HBM),
        slots_near,
        disp_near,
        veloc_near,
        *near[:6],
        spill,
        *near[6:],
    )
    inverse_mass, moved, summed = peer_index, peer_index, peer_index
    for substep in range(SUBSTEPS - 1):
        opening = substep == 0
        extra = [shape((ROWS, LANES))] if opening else []
        outs = pl.pallas_call(
            functools.partial(middle_kernel, opening),
            in_specs=[vector] * 18,
            out_shape=[field, field, field] + extra + sends(3, 4),
            out_specs=[vector] * (7 + len(extra)),
            scratch_shapes=[scratch(4, HALF + 8, LANES)],
            compiler_params=PARAMS,
            name="middle",
        )(
            moved,
            veloc,
            inner,
            *bases,
            summed,
            inverse_mass,
            fixed,
            index,
            collect,
            spread,
            peer_index,
            *got,
            grad,
            back,
        )
        moved, veloc, summed = outs[:3]
        if opening:
            inverse_mass = outs[3]
        got = swap_all(outs[-4:-2], "dev") + swap_all(outs[-2:], "region")
    state = (disp_near, moved, veloc, summed, inverse_mass)
    last_scratch = [
        scratch(2, 4 * FIRST + 8, LANES),
        scratch(2, 3, FIRST * LANES),
        pltpu.SemaphoreType.DMA((2,)),
    ]
    halves = pl.pallas_call(
        inner_last_kernel,
        in_specs=[vector] * 5,
        out_shape=[shape((3, NLOC)), shape((3, NLOC))],
        out_specs=[raw] * 2,
        scratch_shapes=last_scratch,
        compiler_params=PARAMS,
        name="last_inner",
    )(*state)
    return pl.pallas_call(
        edge_last_kernel,
        in_specs=[vector] * 10 + [raw] * 2,
        out_shape=[shape((3, NLOC)), shape((3, NLOC))],
        out_specs=[raw] * 2,
        scratch_shapes=[scratch(4, HALF + 8, LANES)] + last_scratch,
        input_output_aliases={10: 0, 11: 1},
        compiler_params=PARAMS,
        name="last_edge",
    )(*state, peer_index, *got, *halves)


def solution(mesh):
    in_specs = (
        P(None, ("region", "dev")),
        P(None, ("region", "dev")),
        P(None, None, ("region", "dev")),
        P(None, ("region", "dev")),
        P(None, ("region", "dev")),
        P(None, ("region", "dev")),
        P(None, ("region", "dev")),
        P(("region", "dev")),
        P(None, ("region", "dev")),
    )
    out_specs = (P(None, ("region", "dev")), P(None, ("region", "dev")))
    return jax.shard_map(body, mesh=mesh, in_specs=in_specs, out_specs=out_specs, check_vma=False)
```
